512 devices in a mesh: xy: 64 (over z_lo, y, core), gz: 8 (over z_hi, x).
Axes of the slice: x: 4, y: 8, z: 8 (z_hi: 2, z_lo: 4; z = z_hi * 4 + z_lo), core: 2. Of those that a mesh axis runs over, the one named last changes fastest.
Arguments:
- e_check: float32 [3, 512, 16, 1024], P(None, 'xy', 'gz'), may hold values from -6 to 6
- h_check: float32 [3, 512, 16, 1024], P(None, 'xy', 'gz'), may hold values from -6 to 6
- adj_e: float32 [3, 512, 16, 1024], P(None, 'xy', 'gz'), may hold values from -6 to 6
- adj_h: float32 [3, 512, 16, 1024], P(None, 'xy', 'gz'), may hold values from -6 to 6
- material: int32 [512, 16, 1024], P('xy', 'gz'), may hold values from 0 to 3
- owner: int32 [512, 16, 1024], P('xy', 'gz'), may hold values from 0 to 7
- permittivity: float32 [4], replicated, may hold values from 1 to 4
Outputs:
- adj_e_out: float32 [3, 512, 16, 1024], P(None, 'xy', 'gz')
- adj_h_out: float32 [3, 512, 16, 1024], P(None, 'xy', 'gz')
- height_grad: float32 [8], replicated
The draws below stay inside these ranges and needn't reach their ends.
All inputs are finite; a program needn't handle non-finite values.
Results may differ from the reference program's by a relative error of at most 0.0003.
Values sent between devices are 32-bit elements; how exact they have to be, the bound alone decides.
No kernel may reach another device: no remote copies, remote signals or barrier semaphores. Data moves between devices by JAX's collectives and lax.ppermute only.
A program may use at most 64 MiB of HBM per device.

```python
import math
import jax
import jax.numpy as jnp
from jax import lax

NY = 1024
NI = 8
NX = 512
NZ = 16


def plant(entries, own_key, least, top_value):
    spot = [jax.random.randint(jax.random.fold_in(own_key, axis), (), 0, length) for axis, length in enumerate(entries.shape)]
    longest = entries.shape.index(max(entries.shape))
    neighbour = spot[:longest] + [(spot[longest] + 1) % entries.shape[longest]] + spot[longest + 1:]
    return entries.at[tuple(spot)].set(least).at[tuple(neighbour)].set(top_value)


def block_scale(rng, extent, split, least, largest):
    factor_of, own = 1.0, jax.random.fold_in(rng, 6)
    for dim, blocks in split:
        steps = jnp.exp(jax.random.uniform(jax.random.fold_in(own, dim), (blocks,), jnp.float32, least / len(split), largest / len(split)))
        factor_of = factor_of * jnp.repeat(steps, extent[dim] // blocks).reshape([-1 if axis == dim else 1 for axis in range(len(extent))])
    return factor_of


def centred(key, shape, scale, limit, shards=(), dtype=jnp.bfloat16):
    gain = block_scale(key, shape, shards, -0.22, 0.18) if shards else 1.0
    drawn = jax.random.normal(key, shape, jnp.float32) * scale * gain
    return jnp.minimum(jnp.maximum(drawn, -limit), limit).astype(dtype)


def setup_inputs(seed: int = 0) -> dict:
    splits = jax.random.split(jax.random.key(seed), 8)
    return {
        "e_check": centred(splits[0], (3, NX, NZ, NY), 1.0, 6.0, ((1, 64), (2, 8)), jnp.float32),
        "h_check": centred(splits[1], (3, NX, NZ, NY), 1.0, 6.0, ((1, 64), (2, 8)), jnp.float32),
        "adj_e": centred(splits[2], (3, NX, NZ, NY), 1.0, 6.0, ((1, 64), (2, 8)), jnp.float32),
        "adj_h": centred(splits[3], (3, NX, NZ, NY), 1.0, 6.0, ((1, 64), (2, 8)), jnp.float32),
        "material": plant(jax.random.randint(splits[4], (NX, NZ, NY), 0, 4), jax.random.fold_in(splits[4], 1), 0, 3).astype(jnp.int32),
        "owner": plant(jax.random.randint(splits[5], (NX, NZ, NY), 0, NI), jax.random.fold_in(splits[5], 1), 0, NI - 1).astype(jnp.int32),
        "permittivity": jnp.clip(jnp.exp(jax.random.uniform(splits[6], (4,), jnp.float32, math.log(1.0), math.log(4.0))), 1.0, 4.0),
    }


COURANT = 0.5

def diff_ahead(values, dim_axis):
    count = values.shape[dim_axis]
    zero_plane = jnp.zeros_like(lax.slice_in_dim(values, 0, 1, axis=dim_axis))
    later = jnp.concatenate([lax.slice_in_dim(values, 1, count, axis=dim_axis), zero_plane], axis=dim_axis)
    return later - values

def diff_behind(values, dim_axis):
    count = values.shape[dim_axis]
    zero_plane = jnp.zeros_like(lax.slice_in_dim(values, 0, 1, axis=dim_axis))
    earlier = jnp.concatenate([zero_plane, lax.slice_in_dim(values, 0, count - 1, axis=dim_axis)], axis=dim_axis)
    return values - earlier

def curl_with(fields, differ):
    comp_x, comp_y, comp_z = (fields[0], fields[1], fields[2])
    curl_x = differ(comp_z, 2) - differ(comp_y, 1)
    curl_y = differ(comp_x, 1) - differ(comp_z, 0)
    curl_z = differ(comp_y, 0) - differ(comp_x, 2)
    return jnp.stack([curl_x, curl_y, curl_z], axis=0)

def reference(e_check, h_check, adj_e, adj_h, material, owner, permittivity):
    e_coef = COURANT / permittivity[material]
    electric = [e_check]
    magnetic = h_check
    for index_step in range(2):
        magnetic = magnetic - COURANT * curl_with(electric[-1], diff_ahead)
        electric.append(electric[-1] + e_coef * curl_with(magnetic, diff_behind))
    adjoint_e, adjoint_h = (adj_e, adj_h)
    gradient = jnp.zeros((NI,), jnp.float32)
    for later_step in (2, 1):
        weight = e_coef * lax.optimization_barrier(jnp.sum(adjoint_e * (electric[later_step] - electric[later_step - 1]), axis=0))
        gradient = gradient + jax.ops.segment_sum(weight.reshape(-1), owner.reshape(-1).astype(jnp.int32), num_segments=NI)
        adjoint_h = adjoint_h + curl_with(e_coef * adjoint_e, diff_ahead)
        adjoint_e = adjoint_e - COURANT * curl_with(adjoint_h, diff_behind)
    total_cells = NX * NZ * NY
    gradient = gradient / jnp.sqrt(jnp.float32(total_cells / NI))
    return (adjoint_e, adjoint_h, gradient)
```

```python
import functools

import jax
import jax.numpy as jnp
from jax import lax
from jax.experimental import pallas as pl
from jax.experimental.pallas import tpu as pltpu
from jax.sharding import Mesh
from jax.sharding import PartitionSpec as P

NI = 8
AXES = ("zl", "y", "c", "zh", "x")
XY = ("zl", "y", "c")
GZ = ("zh", "x")
COURANT = 0.5
ALPHA = (-COURANT, 1.0)
BETA = (1.0, -COURANT)

UP_LINES = (("ax", 10), ("ay", 10), ("px", 8), ("py", 8))
DOWN_LINES = (("sx", 11), ("sy", 10), ("qx", 9), ("qy", 8))
LINES = 2 * 38 + 9
HALO = 26


def shift_later(u):
    lane = lax.broadcasted_iota(jnp.int32, u.shape, u.ndim - 1)
    row = lax.broadcasted_iota(jnp.int32, u.shape, u.ndim - 2)
    turned = pltpu.roll(u, 127, u.ndim - 1)
    carried = pltpu.roll(turned, 7, u.ndim - 2)
    return jnp.where(lane < 127, turned, jnp.where(row < 7, carried, 0.0))


def shift_earlier(u):
    lane = lax.broadcasted_iota(jnp.int32, u.shape, u.ndim - 1)
    row = lax.broadcasted_iota(jnp.int32, u.shape, u.ndim - 2)
    turned = pltpu.roll(u, 1, u.ndim - 1)
    carried = pltpu.roll(turned, 1, u.ndim - 2)
    return jnp.where(lane > 0, turned, jnp.where(row > 0, carried, 0.0))


def ahead_y(u):
    return shift_later(u) - u


def behind_y(u):
    return u - shift_earlier(u)


def table(material, values):
    out = jnp.zeros(material.shape, jnp.float32)
    for kind in range(4):
        out = out + jnp.where(material == kind, values[kind], 0.0)
    return out


def coefs(eps_ref):
    return [COURANT / eps_ref[kind] for kind in range(4)]


def plane(z):
    return pl.ds(z, 8, stride=2)


def keep_low(u, count, flag):
    return jnp.concatenate([u[:count] * flag, u[count:]], axis=0)


def low_flag(axes):
    first = functools.reduce(jnp.logical_and, [lax.axis_index(a) == 0 for a in axes])
    return jnp.where(first, 0.0, 1.0).astype(jnp.float32)


def pack_kernel(eps_ref, e0, e1, h0, h1, g0, g1, k0, k1, m0, m1, pair_ref, next_ref):
    even = lax.axis_index("c") == 0
    values = coefs(eps_ref)

    def put(row, first, last):
        pair_ref[row] = jnp.where(even, last, first)
        next_ref[row] = jnp.where(even, first, last)

    for field, (first, last) in enumerate(((e0, e1), (h0, h1), (g0, g1), (k0, k1))):
        for comp in range(3):
            for k in range(2):
                put(field * 6 + comp * 2 + k, first[comp, k], last[comp, k])
    for k in range(2):
        put(24 + k, table(m0[k], values), table(m1[k], values))


def local_kernel(eps_ref, e, h, g, kf, m, pair_ref, next_ref, pay0, pay1, t1s, s1s, s0s, cs):
    even_x = lax.axis_index("c") == 0
    even_z = lax.axis_index("x") % 2 == 0
    x_flag = low_flag(XY)
    values = coefs(eps_ref)

    def below(row, z):
        return jnp.where(even_x, next_ref[row, plane(z), :], pair_ref[row, plane(z), :])[None]

    def above(row, z):
        return jnp.where(even_x, pair_ref[row, plane(z), :], next_ref[row, plane(z), :])[None]

    def extended(ref, base, comp, z):
        row = base + comp * 2
        return jnp.concatenate(
            [below(row, z), below(row + 1, z), ref[comp, :, plane(z), :], above(row, z), above(row + 1, z)],
            axis=0,
        )

    coef = []
    for z in range(2):
        own = table(m[:, plane(z), :], values)
        coef.append(jnp.concatenate([below(24, z), below(25, z), own, above(24, z), above(25, z)], axis=0))
        cs[z] = coef[z][1:11]

    def put(row, up, down):
        pay0[row] = jnp.where(even_z, up, down)
        pay1[row] = jnp.where(even_z, down, up)

    for chain in range(2):
        alpha, beta = ALPHA[chain], BETA[chain]
        if chain == 0:
            s = [[extended(e, 0, comp, z) for z in range(2)] for comp in range(3)]
            t = [[extended(h, 6, comp, z)[:11] for z in range(2)] for comp in range(3)]
        else:
            s = [[extended(g, 12, comp, z) * coef[z] for z in range(2)] for comp in range(3)]
            t = [[extended(kf, 18, comp, z)[:11] for z in range(2)] for comp in range(3)]
        sx, sy, sz = s
        t1 = [[None, None] for _ in range(3)]
        for z in range(2):
            dz_y = (sy[1] - sy[0])[:11] if z == 0 else -sy[1][:11]
            dz_x = (sx[1] - sx[0])[:11] if z == 0 else -sx[1][:11]
            t1[0][z] = t[0][z] + alpha * (ahead_y(sz[z][:11]) - dz_y)
            t1[1][z] = t[1][z] + alpha * (dz_x - (sz[z][1:] - sz[z][:11]))
            t1[2][z] = t[2][z] + alpha * ((sy[z][1:] - sy[z][:11]) - ahead_y(sx[z][:11]))
            for comp in range(3):
                t1[comp][z] = keep_low(t1[comp][z], 2, x_flag)
                t1s[chain, comp, z] = t1[comp][z]
        s1 = [[None, None] for _ in range(3)]
        for z in range(2):
            tx, ty, tz = t1[0][z], t1[1][z], t1[2][z]
            b = beta * coef[z][1:11]
            dz_y = ty[1:] if z == 0 else (ty - t1[1][0])[1:]
            dz_x = tx[1:] if z == 0 else (tx - t1[0][0])[1:]
            s1[0][z] = sx[z][1:11] + b * (behind_y(tz[1:]) - dz_y)
            s1[1][z] = sy[z][1:11] + b * (dz_x - (tz[1:] - tz[:10]))
            s1[2][z] = sz[z][1:11] + b * ((ty[1:] - ty[:10]) - behind_y(tx[1:]))
            for comp in range(3):
                s1s[chain, comp, z] = s1[comp][z]
        s0s[chain, 0] = sx[0][1:11]
        s0s[chain, 1] = sy[0][1:11]
        ax, ay = t1[0][1][1:], t1[1][1][1:]
        px = ax[1:9] + alpha * (ahead_y(s1[2][1][1:9]) + s1[1][1][1:9])
        py = ay[1:9] - alpha * (s1[0][1][1:9] + (s1[2][1][2:10] - s1[2][1][1:9]))
        up = jnp.concatenate([ax, ay, px, py, jnp.zeros((2, 8, 128), jnp.float32)], axis=0)
        down = jnp.concatenate([sx[0][:11], sy[0][1:11], s1[0][0][:9], s1[1][0][1:9]], axis=0)
        put(pl.ds(38 * chain, 38), up, down)
    put(pl.ds(76, 9), coef[1][2:11], coef[0][1:10])


def final_kernel(eps_ref, e, g, m, owner, r0, r1, t1s, s1s, s0s, cs, adj_e, adj_h, sums):
    even_z = lax.axis_index("x") % 2 == 0
    x_flag, z_flag = low_flag(XY), low_flag(GZ)
    values = coefs(eps_ref)
    inverse = [2.0 * eps_ref[kind] for kind in range(4)]

    def above(start, count):
        return jnp.where(even_z, r0[pl.ds(start, count)], r1[pl.ds(start, count)])

    def below(start, count):
        return jnp.where(even_z, r1[pl.ds(start, count)], r0[pl.ds(start, count)])

    c_up, c_low = above(76, 9), below(76, 9)
    own = slice(1, 9)
    kept = []
    for chain in range(2):
        alpha, beta = ALPHA[chain], BETA[chain]
        base = 38 * chain
        sx2, sy2, qx, qy = above(base, 11), above(base + 11, 10), above(base + 21, 9), above(base + 30, 8)
        ax, ay, px, py = below(base, 10), below(base + 10, 10), below(base + 20, 8), below(base + 28, 8)
        sx0, sy0 = s0s[chain, 0], s0s[chain, 1]
        tx = [t1s[chain, 0, 0][1:], t1s[chain, 0, 1][1:] - alpha * sy2]
        ty = [t1s[chain, 1, 0][1:], t1s[chain, 1, 1][1:] + alpha * sx2[1:]]
        tz = [t1s[chain, 2, 0][1:], t1s[chain, 2, 1][1:]]
        tx_low = (ax - alpha * sy0) * z_flag
        ty_low = (ay + alpha * sx0) * z_flag
        b0, b1 = beta * cs[0], beta * cs[1]
        div2 = (sx2[1:] - sx2[:10]) + behind_y(sy2)
        sx = [s1s[chain, 0, 0] + b0 * ty_low, s1s[chain, 0, 1] - alpha * b1 * sx2[1:]]
        sy = [s1s[chain, 1, 0] - b0 * tx_low, s1s[chain, 1, 1] - alpha * b1 * sy2]
        sz = [s1s[chain, 2, 0], s1s[chain, 2, 1] + alpha * b1 * div2]
        b_up, b_low = beta * c_up, beta * c_low
        sx.append(qx + b_up * ty[1][:9])
        sy_top = qy - b_up[1:] * tx[1][own]
        t2x, t2y, t2z = [], [], []
        for z in range(2):
            dz_y = (sy[1] - sy[0])[own] if z == 0 else sy_top - sy[1][own]
            dz_x = sx[z + 1][:9] - sx[z][:9]
            t2x.append(tx[z][own] + alpha * (ahead_y(sz[z][own]) - dz_y))
            y_new = ty[z][:9] + alpha * (dz_x - (sz[z][1:] - sz[z][:9]))
            z_new = tz[z][:9] + alpha * ((sy[z][1:] - sy[z][:9]) - ahead_y(sx[z][:9]))
            t2y.append(keep_low(y_new, 1, x_flag))
            t2z.append(keep_low(z_new, 1, x_flag))
        div0 = b_low * ((sx0[1:] - sx0[:9]) + behind_y(sy0[1:]))
        x_low = px - alpha * (sy0[own] + sy[0][own]) + alpha * alpha * (ahead_y(div0[:8]) - b_low[:8] * sy0[own])
        y_low = py + alpha * (sx0[own] + sx[0][own]) + alpha * alpha * (b_low[:8] * sx0[own] - (div0[1:] - div0[:8]))
        x_low, y_low = x_low * z_flag, y_low * z_flag
        curl = []
        for z in range(2):
            dz_y = t2y[z][1:] - (y_low if z == 0 else t2y[0][1:])
            dz_x = t2x[z] - (x_low if z == 0 else t2x[0])
            curl.append((
                behind_y(t2z[z][1:]) - dz_y,
                dz_x - (t2z[z][1:] - t2z[z][:8]),
                (t2y[z][1:] - t2y[z][:8]) - behind_y(t2x[z]),
            ))
        kept.append(([[s[z][own] for s in (sx, sy, sz)] for z in range(2)], curl))
        if chain == 1:
            for z in range(2):
                scale = table(m[:, plane(z), :], inverse)
                for comp, t2 in enumerate((t2x[z], t2y[z][1:], t2z[z][1:])):
                    adj_e[comp, :, plane(z), :] = kept[1][0][z][comp] * scale - COURANT * curl[z][comp]
                    adj_h[comp, :, plane(z), :] = t2

    totals = [jnp.zeros((8, 128), jnp.float32) for _ in range(NI)]
    for z in range(2):
        coef = table(m[:, plane(z), :], values)
        weight = jnp.zeros((8, 8, 128), jnp.float32)
        for comp in range(3):
            step = kept[0][0][z][comp] - e[comp, :, plane(z), :]
            weight = weight + kept[1][0][z][comp] * step
            weight = weight + coef * g[comp, :, plane(z), :] * (coef * kept[0][1][z][comp])
        who = owner[:, plane(z), :]
        for j in range(NI):
            totals[j] = totals[j] + jnp.sum(jnp.where(who == j, weight, 0.0), axis=0)
    lane = lax.broadcasted_iota(jnp.int32, (1, 128), 1)
    row = jnp.zeros((1, 128), jnp.float32)
    for j in range(NI):
        row = row + jnp.where(lane == j, jnp.sum(totals[j]), 0.0)
    sums[...] = jnp.broadcast_to(row, sums.shape)


VMEM = pl.BlockSpec(memory_space=pltpu.VMEM)
SMEM = pl.BlockSpec(memory_space=pltpu.SMEM)
PARAMS = pltpu.CompilerParams(vmem_limit_bytes=48 * 1024 * 1024)


def f32(*shape):
    return jax.ShapeDtypeStruct(shape, jnp.float32)


def rows(u):
    lead = u.shape[:-2]
    n = len(lead)
    return u.reshape(*lead, 2, 8, 128).transpose(*range(n), n + 1, n, n + 2).reshape(*lead, 16, 128)


def unrows(u):
    lead = u.shape[:-2]
    n = len(lead)
    return u.reshape(*lead, 8, 2, 128).transpose(*range(n), n + 1, n, n + 2).reshape(*lead, 2, 1024)


def swap_pairs(value, axes, odd):
    size = lax.axis_size(axes)
    pairs = []
    for low in range(odd, size - 1, 2):
        pairs += [(low, low + 1), (low + 1, low)]
    return lax.ppermute(value, axes, pairs)


def spread_sum(value, axes):
    size = lax.axis_size(axes)
    sent = jnp.broadcast_to(value[None], (size, value.shape[0]))
    return jnp.sum(lax.all_to_all(sent, axes, 0, 0), axis=0)


def body(e_check, h_check, adj_e, adj_h, material, owner, permittivity):
    e, h, g, k, m, own = (rows(u) for u in (e_check, h_check, adj_e, adj_h, material, owner))
    first = pl.BlockSpec((3, 2, 16, 128), lambda i: (0, 0, 0, 0))
    last = pl.BlockSpec((3, 2, 16, 128), lambda i: (0, 3, 0, 0))
    pair, following = pl.pallas_call(
        pack_kernel,
        grid=(1,),
        out_shape=(f32(HALO, 16, 128), f32(HALO, 16, 128)),
        in_specs=[SMEM] + [first, last] * 4
        + [pl.BlockSpec((2, 16, 128), lambda i: (0, 0, 0)), pl.BlockSpec((2, 16, 128), lambda i: (3, 0, 0))],
        out_specs=[pl.BlockSpec((HALO, 16, 128), lambda i: (0, 0, 0))] * 2,
        compiler_params=PARAMS,
        name="pack",
    )(permittivity, e, e, h, h, g, g, k, k, m, m)
    following = swap_pairs(following, XY, 1)
    pair = swap_pairs(pair, "c", 0)
    pay0, pay1, t1s, s1s, s0s, cs = pl.pallas_call(
        local_kernel,
        out_shape=(
            f32(LINES, 8, 128),
            f32(LINES, 8, 128),
            f32(2, 3, 2, 11, 8, 128),
            f32(2, 3, 2, 10, 8, 128),
            f32(2, 2, 10, 8, 128),
            f32(2, 10, 8, 128),
        ),
        in_specs=[SMEM] + [VMEM] * 7,
        out_specs=[VMEM] * 6,
        compiler_params=PARAMS,
        name="local_step",
    )(permittivity, e, h, g, k, m, pair, following)
    pay1 = swap_pairs(pay1, GZ, 1)
    pay0 = swap_pairs(pay0, "x", 0)
    out_e, out_h, sums = pl.pallas_call(
        final_kernel,
        out_shape=(f32(3, 8, 16, 128), f32(3, 8, 16, 128), f32(1, 128)),
        in_specs=[SMEM] + [VMEM] * 10,
        out_specs=[VMEM] * 3,
        compiler_params=PARAMS,
        name="final_step",
    )(permittivity, e, g, m, own, pay0, pay1, t1s, s1s, s0s, cs)
    total = spread_sum(sums[0], ("zl", "zh", "c"))
    total = spread_sum(total, ("y", "x"))
    cells = 8 * lax.axis_size(XY) * 2 * lax.axis_size(GZ) * 1024
    gradient = total[:NI] / jnp.sqrt(jnp.float32(cells / NI))
    return unrows(out_e), unrows(out_h), gradient


def on_split(split):
    return jax.shard_map(
        body,
        mesh=split,
        in_specs=(P(None, XY, GZ, None),) * 4 + (P(XY, GZ, None),) * 2 + (P(),),
        out_specs=(P(None, XY, GZ, None), P(None, XY, GZ, None), P()),
        check_vma=False,
    )


def solution(mesh):
    return on_split(Mesh(mesh.devices.reshape(4, 8, 2, 2, 4), AXES))
```

```python
import functools

import jax
import jax.numpy as jnp
from jax import lax
from jax.experimental import pallas as pl
from jax.experimental.pallas import tpu as pltpu
from jax.sharding import Mesh
from jax.sharding import PartitionSpec as P

NI = 8
AXES = ("zl", "y", "c", "zh", "x")
XY = ("zl", "y", "c")
GZ = ("zh", "x")
COURANT = 0.5
ALPHA = (-COURANT, 1.0)
BETA = (1.0, -COURANT)

UP_LINES = (("ax", 10), ("ay", 10), ("px", 8), ("py", 8))
DOWN_LINES = (("sx", 11), ("sy", 10), ("qx", 9), ("qy", 8))
LINES = 2 * 38 + 9
HALO = 26


def shift_later(u):
    lane = lax.broadcasted_iota(jnp.int32, u.shape, u.ndim - 1)
    row = lax.broadcasted_iota(jnp.int32, u.shape, u.ndim - 2)
    turned = pltpu.roll(u, 127, u.ndim - 1)
    carried = pltpu.roll(turned, 7, u.ndim - 2)
    return jnp.where(lane < 127, turned, jnp.where(row < 7, carried, 0.0))


def shift_earlier(u):
    lane = lax.broadcasted_iota(jnp.int32, u.shape, u.ndim - 1)
    row = lax.broadcasted_iota(jnp.int32, u.shape, u.ndim - 2)
    turned = pltpu.roll(u, 1, u.ndim - 1)
    carried = pltpu.roll(turned, 1, u.ndim - 2)
    return jnp.where(lane > 0, turned, jnp.where(row > 0, carried, 0.0))


def ahead_y(u):
    return shift_later(u) - u


def behind_y(u):
    return u - shift_earlier(u)


def table(material, values):
    out = jnp.zeros(material.shape, jnp.float32)
    for kind in range(4):
        out = out + jnp.where(material == kind, values[kind], 0.0)
    return out


def coefs(eps_ref):
    return [COURANT / eps_ref[kind] for kind in range(4)]


def plane(z):
    return pl.ds(z, 8, stride=2)


def keep_low(u, count, flag):
    return jnp.concatenate([u[:count] * flag, u[count:]], axis=0)


def low_flag(axes):
    first = functools.reduce(jnp.logical_and, [lax.axis_index(a) == 0 for a in axes])
    return jnp.where(first, 0.0, 1.0).astype(jnp.float32)


def pack_kernel(eps_ref, e, h, g, k, m, pair_ref, next_ref, eps, strips, kinds, sems):
    copies = [pltpu.make_async_copy(eps_ref, eps, sems.at[10])]
    for side, start in enumerate((0, 6)):
        for field, ref in enumerate((e, h, g, k)):
            copies.append(
                pltpu.make_async_copy(ref.at[:, start : start + 2], strips.at[side, field], sems.at[side * 5 + field])
            )
        copies.append(pltpu.make_async_copy(m.at[start : start + 2], kinds.at[side], sems.at[side * 5 + 4]))
    for copy in copies:
        copy.start()
    for copy in copies:
        copy.wait()
    even = lax.axis_index("c") == 0
    values = coefs(eps)

    def put(row, first, last):
        pair_ref[row] = jnp.where(even, last, first)
        next_ref[row] = jnp.where(even, first, last)

    for field in range(4):
        for comp in range(3):
            for line in range(2):
                put(field * 6 + comp * 2 + line, strips[0, field, comp, line], strips[1, field, comp, line])
    for line in range(2):
        put(24 + line, table(kinds[0, line], values), table(kinds[1, line], values))


def local_kernel(eps_ref, e, h, g, kf, m, next_ref, pair_ref, pay0, pay1, t1s, s1s, s0s, cs):
    even_x = lax.axis_index("c") == 0
    even_z = lax.axis_index("x") % 2 == 0
    x_flag = low_flag(XY)
    values = coefs(eps_ref)

    def below(row, z):
        return jnp.where(even_x, next_ref[row, plane(z), :], pair_ref[row, plane(z), :])[None]

    def above(row, z):
        return jnp.where(even_x, pair_ref[row, plane(z), :], next_ref[row, plane(z), :])[None]

    def extended(ref, base, comp, z):
        row = base + comp * 2
        return jnp.concatenate(
            [below(row, z), below(row + 1, z), ref[comp, :, plane(z), :], above(row, z), above(row + 1, z)],
            axis=0,
        )

    coef = []
    for z in range(2):
        own = table(m[:, plane(z), :], values)
        coef.append(jnp.concatenate([below(24, z), below(25, z), own, above(24, z), above(25, z)], axis=0))
        cs[z] = coef[z][1:11]

    def put(row, up, down):
        pay0[row] = jnp.where(even_z, up, down)
        pay1[row] = jnp.where(even_z, down, up)

    for chain in range(2):
        alpha, beta = ALPHA[chain], BETA[chain]
        if chain == 0:
            s = [[extended(e, 0, comp, z) for z in range(2)] for comp in range(3)]
            t = [[extended(h, 6, comp, z)[:11] for z in range(2)] for comp in range(3)]
        else:
            s = [[extended(g, 12, comp, z) * coef[z] for z in range(2)] for comp in range(3)]
            t = [[extended(kf, 18, comp, z)[:11] for z in range(2)] for comp in range(3)]
        sx, sy, sz = s
        t1 = [[None, None] for _ in range(3)]
        for z in range(2):
            dz_y = (sy[1] - sy[0])[:11] if z == 0 else -sy[1][:11]
            dz_x = (sx[1] - sx[0])[:11] if z == 0 else -sx[1][:11]
            t1[0][z] = t[0][z] + alpha * (ahead_y(sz[z][:11]) - dz_y)
            t1[1][z] = t[1][z] + alpha * (dz_x - (sz[z][1:] - sz[z][:11]))
            t1[2][z] = t[2][z] + alpha * ((sy[z][1:] - sy[z][:11]) - ahead_y(sx[z][:11]))
            for comp in range(3):
                t1[comp][z] = keep_low(t1[comp][z], 2, x_flag)
                t1s[chain, comp, z] = t1[comp][z]
        s1 = [[None, None] for _ in range(3)]
        for z in range(2):
            tx, ty, tz = t1[0][z], t1[1][z], t1[2][z]
            b = beta * coef[z][1:11]
            dz_y = ty[1:] if z == 0 else (ty - t1[1][0])[1:]
            dz_x = tx[1:] if z == 0 else (tx - t1[0][0])[1:]
            s1[0][z] = sx[z][1:11] + b * (behind_y(tz[1:]) - dz_y)
            s1[1][z] = sy[z][1:11] + b * (dz_x - (tz[1:] - tz[:10]))
            s1[2][z] = sz[z][1:11] + b * ((ty[1:] - ty[:10]) - behind_y(tx[1:]))
            for comp in range(3):
                s1s[chain, comp, z] = s1[comp][z]
        s0s[chain, 0] = sx[0][1:11]
        s0s[chain, 1] = sy[0][1:11]
        ax, ay = t1[0][1][1:], t1[1][1][1:]
        px = ax[1:9] + alpha * (ahead_y(s1[2][1][1:9]) + s1[1][1][1:9])
        py = ay[1:9] - alpha * (s1[0][1][1:9] + (s1[2][1][2:10] - s1[2][1][1:9]))
        up = jnp.concatenate([ax, ay, px, py, jnp.zeros((2, 8, 128), jnp.float32)], axis=0)
        down = jnp.concatenate([sx[0][:11], sy[0][1:11], s1[0][0][:9], s1[1][0][1:9]], axis=0)
        put(pl.ds(38 * chain, 38), up, down)
    put(pl.ds(76, 9), coef[1][2:11], coef[0][1:10])


def final_kernel(eps_ref, e, g, m, owner, r1, r0, t1s, s1s, s0s, cs, adj_e, adj_h, sums):
    even_z = lax.axis_index("x") % 2 == 0
    x_flag, z_flag = low_flag(XY), low_flag(GZ)
    values = coefs(eps_ref)
    inverse = [2.0 * eps_ref[kind] for kind in range(4)]

    def above(start, count):
        return jnp.where(even_z, r0[pl.ds(start, count)], r1[pl.ds(start, count)])

    def below(start, count):
        return jnp.where(even_z, r1[pl.ds(start, count)], r0[pl.ds(start, count)])

    c_up, c_low = above(76, 9), below(76, 9)
    own = slice(1, 9)
    kept = []
    for chain in range(2):
        alpha, beta = ALPHA[chain], BETA[chain]
        base = 38 * chain
        sx2, sy2, qx, qy = above(base, 11), above(base + 11, 10), above(base + 21, 9), above(base + 30, 8)
        ax, ay, px, py = below(base, 10), below(base + 10, 10), below(base + 20, 8), below(base + 28, 8)
        sx0, sy0 = s0s[chain, 0], s0s[chain, 1]
        tx = [t1s[chain, 0, 0][1:], t1s[chain, 0, 1][1:] - alpha * sy2]
        ty = [t1s[chain, 1, 0][1:], t1s[chain, 1, 1][1:] + alpha * sx2[1:]]
        tz = [t1s[chain, 2, 0][1:], t1s[chain, 2, 1][1:]]
        tx_low = (ax - alpha * sy0) * z_flag
        ty_low = (ay + alpha * sx0) * z_flag
        b0, b1 = beta * cs[0], beta * cs[1]
        div2 = (sx2[1:] - sx2[:10]) + behind_y(sy2)
        sx = [s1s[chain, 0, 0] + b0 * ty_low, s1s[chain, 0, 1] - alpha * b1 * sx2[1:]]
        sy = [s1s[chain, 1, 0] - b0 * tx_low, s1s[chain, 1, 1] - alpha * b1 * sy2]
        sz = [s1s[chain, 2, 0], s1s[chain, 2, 1] + alpha * b1 * div2]
        b_up, b_low = beta * c_up, beta * c_low
        sx.append(qx + b_up * ty[1][:9])
        sy_top = qy - b_up[1:] * tx[1][own]
        t2x, t2y, t2z = [], [], []
        for z in range(2):
            dz_y = (sy[1] - sy[0])[own] if z == 0 else sy_top - sy[1][own]
            dz_x = sx[z + 1][:9] - sx[z][:9]
            t2x.append(tx[z][own] + alpha * (ahead_y(sz[z][own]) - dz_y))
            y_new = ty[z][:9] + alpha * (dz_x - (sz[z][1:] - sz[z][:9]))
            z_new = tz[z][:9] + alpha * ((sy[z][1:] - sy[z][:9]) - ahead_y(sx[z][:9]))
            t2y.append(keep_low(y_new, 1, x_flag))
            t2z.append(keep_low(z_new, 1, x_flag))
        div0 = b_low * ((sx0[1:] - sx0[:9]) + behind_y(sy0[1:]))
        x_low = px - alpha * (sy0[own] + sy[0][own]) + alpha * alpha * (ahead_y(div0[:8]) - b_low[:8] * sy0[own])
        y_low = py + alpha * (sx0[own] + sx[0][own]) + alpha * alpha * (b_low[:8] * sx0[own] - (div0[1:] - div0[:8]))
        x_low, y_low = x_low * z_flag, y_low * z_flag
        curl = []
        for z in range(2):
            dz_y = t2y[z][1:] - (y_low if z == 0 else t2y[0][1:])
            dz_x = t2x[z] - (x_low if z == 0 else t2x[0])
            curl.append((
                behind_y(t2z[z][1:]) - dz_y,
                dz_x - (t2z[z][1:] - t2z[z][:8]),
                (t2y[z][1:] - t2y[z][:8]) - behind_y(t2x[z]),
            ))
        kept.append(([[s[z][own] for s in (sx, sy, sz)] for z in range(2)], curl))
        if chain == 1:
            for z in range(2):
                scale = table(m[:, plane(z), :], inverse)
                for comp, t2 in enumerate((t2x[z], t2y[z][1:], t2z[z][1:])):
                    adj_e[comp, :, plane(z), :] = kept[1][0][z][comp] * scale - COURANT * curl[z][comp]
                    adj_h[comp, :, plane(z), :] = t2

    totals = [jnp.zeros((8, 128), jnp.float32) for _ in range(NI)]
    for z in range(2):
        coef = table(m[:, plane(z), :], values)
        weight = jnp.zeros((8, 8, 128), jnp.float32)
        for comp in range(3):
            step = kept[0][0][z][comp] - e[comp, :, plane(z), :]
            weight = weight + kept[1][0][z][comp] * step
            weight = weight + coef * g[comp, :, plane(z), :] * (coef * kept[0][1][z][comp])
        who = owner[:, plane(z), :]
        for j in range(NI):
            totals[j] = totals[j] + jnp.sum(jnp.where(who == j, weight, 0.0), axis=0)
    lane = lax.broadcasted_iota(jnp.int32, (1, 128), 1)
    row = jnp.zeros((1, 128), jnp.float32)
    for j in range(NI):
        row = row + jnp.where(lane == j, jnp.sum(totals[j]), 0.0)
    sums[...] = jnp.broadcast_to(row, sums.shape)


VMEM = pl.BlockSpec(memory_space=pltpu.VMEM)
SMEM = pl.BlockSpec(memory_space=pltpu.SMEM)
HBM = pl.BlockSpec(memory_space=pltpu.HBM)
LARGE = 62 * 1024 * 1024
PARAMS = pltpu.CompilerParams(vmem_limit_bytes=48 * 1024 * 1024)


def f32(*shape):
    return jax.ShapeDtypeStruct(shape, jnp.float32)


def rows(u):
    lead = u.shape[:-2]
    n = len(lead)
    return u.reshape(*lead, 2, 8, 128).transpose(*range(n), n + 1, n, n + 2).reshape(*lead, 16, 128)


def unrows(u):
    lead = u.shape[:-2]
    n = len(lead)
    return u.reshape(*lead, 8, 2, 128).transpose(*range(n), n + 1, n, n + 2).reshape(*lead, 2, 1024)


def swap_pairs(value, axes, odd):
    size = lax.axis_size(axes)
    pairs = []
    for low in range(odd, size - 1, 2):
        pairs += [(low, low + 1), (low + 1, low)]
    return lax.ppermute(value, axes, pairs)


def spread_sum(value, axes):
    size = lax.axis_size(axes)
    sent = jnp.broadcast_to(value[None], (size, value.shape[0]))
    return jnp.sum(lax.all_to_all(sent, axes, 0, 0), axis=0)


def body(e_check, h_check, adj_e, adj_h, material, owner, permittivity):
    e, h, g, k, m, own = (rows(u) for u in (e_check, h_check, adj_e, adj_h, material, owner))
    pair, following = pl.pallas_call(
        pack_kernel,
        out_shape=(f32(HALO, 16, 128), f32(HALO, 16, 128)),
        in_specs=[HBM] * 6,
        out_specs=[VMEM] * 2,
        scratch_shapes=[
            pltpu.SMEM((4,), jnp.float32),
            pltpu.VMEM((2, 4, 3, 2, 16, 128), jnp.float32),
            pltpu.VMEM((2, 2, 16, 128), jnp.int32),
            pltpu.SemaphoreType.DMA((11,)),
        ],
        compiler_params=pltpu.CompilerParams(vmem_limit_bytes=LARGE),
        name="pack",
    )(permittivity, e, h, g, k, m)
    pair = swap_pairs(pair, "c", 0)
    following = swap_pairs(following, XY, 1)
    pay0, pay1, t1s, s1s, s0s, cs = pl.pallas_call(
        local_kernel,
        out_shape=(
            f32(LINES, 8, 128),
            f32(LINES, 8, 128),
            f32(2, 3, 2, 11, 8, 128),
            f32(2, 3, 2, 10, 8, 128),
            f32(2, 2, 10, 8, 128),
            f32(2, 10, 8, 128),
        ),
        in_specs=[SMEM] + [VMEM] * 7,
        out_specs=[VMEM] * 6,
        compiler_params=PARAMS,
        name="local_step",
    )(permittivity, e, h, g, k, m, following, pair)
    pay0 = swap_pairs(pay0, "x", 0)
    pay1 = swap_pairs(pay1, GZ, 1)
    out_e, out_h, sums = pl.pallas_call(
        final_kernel,
        out_shape=(f32(3, 8, 16, 128), f32(3, 8, 16, 128), f32(1, 128)),
        in_specs=[SMEM] + [VMEM] * 10,
        out_specs=[VMEM] * 3,
        compiler_params=PARAMS,
        name="final_step",
    )(permittivity, e, g, m, own, pay1, pay0, t1s, s1s, s0s, cs)
    total = spread_sum(sums[0], ("zl", "zh", "c"))
    total = spread_sum(total, ("y", "x"))
    cells = 8 * lax.axis_size(XY) * 2 * lax.axis_size(GZ) * 1024
    gradient = total[:NI] / jnp.sqrt(jnp.float32(cells / NI))
    return unrows(out_e), unrows(out_h), gradient


def on_split(split):
    return jax.shard_map(
        body,
        mesh=split,
        in_specs=(P(None, XY, GZ, None),) * 4 + (P(XY, GZ, None),) * 2 + (P(),),
        out_specs=(P(None, XY, GZ, None), P(None, XY, GZ, None), P()),
        check_vma=False,
    )


def solution(mesh):
    return on_split(Mesh(mesh.devices.reshape(4, 8, 2, 2, 4), AXES))
```

```python
import functools

import jax
import jax.numpy as jnp
from jax import lax
from jax.experimental import pallas as pl
from jax.experimental.pallas import tpu as pltpu
from jax.sharding import Mesh
from jax.sharding import PartitionSpec as P

NI = 8
AXES = ("zl", "y", "c", "zh", "x")
XY = ("zl", "y", "c")
GZ = ("zh", "x")
COURANT = 0.5
ALPHA = (-COURANT, 1.0)
BETA = (1.0, -COURANT)

UP = (("ax", 10, 1, 1), ("ay", 10, 1, 2), ("px", 8, 1, 1), ("py", 8, 1, 2))
DOWN = (("sx", 11, 2, 1), ("sy", 10, 1, 1), ("qx", 9, 1, 1), ("qy", 8, 1, 1))
EARLY = 2 * 29 + 8
LATE = 2 * 10 + 1
HALO = 26


def shift_later(u):
    lane = lax.broadcasted_iota(jnp.int32, u.shape, u.ndim - 1)
    row = lax.broadcasted_iota(jnp.int32, u.shape, u.ndim - 2)
    turned = pltpu.roll(u, 127, u.ndim - 1)
    carried = pltpu.roll(turned, 7, u.ndim - 2)
    return jnp.where(lane < 127, turned, jnp.where(row < 7, carried, 0.0))


def shift_earlier(u):
    lane = lax.broadcasted_iota(jnp.int32, u.shape, u.ndim - 1)
    row = lax.broadcasted_iota(jnp.int32, u.shape, u.ndim - 2)
    turned = pltpu.roll(u, 1, u.ndim - 1)
    carried = pltpu.roll(turned, 1, u.ndim - 2)
    return jnp.where(lane > 0, turned, jnp.where(row > 0, carried, 0.0))


def ahead_y(u):
    return shift_later(u) - u


def behind_y(u):
    return u - shift_earlier(u)


def table(material, values):
    out = jnp.zeros(material.shape, jnp.float32)
    for kind in range(4):
        out = out + jnp.where(material == kind, values[kind], 0.0)
    return out


def coefs(eps_ref):
    return [COURANT / eps_ref[kind] for kind in range(4)]


def plane(z):
    return pl.ds(z, 8, stride=2)


def keep_low(u, count, flag):
    return jnp.concatenate([u[:count] * flag, u[count:]], axis=0)


def low_flag(axes):
    first = functools.reduce(jnp.logical_and, [lax.axis_index(a) == 0 for a in axes])
    return jnp.where(first, 0.0, 1.0).astype(jnp.float32)


def pack_kernel(eps_ref, e, h, g, k, m, pair_ref, next_ref, early0, early1, eps, fields, kinds, sems):
    copies = [pltpu.make_async_copy(eps_ref, eps, sems.at[5]), pltpu.make_async_copy(m, kinds, sems.at[4])]
    for field, ref in enumerate((e, h, g, k)):
        copies.append(pltpu.make_async_copy(ref, fields.at[field], sems.at[field]))
    for copy in copies:
        copy.start()
    for copy in copies:
        copy.wait()
    even = lax.axis_index("c") == 0
    even_z = lax.axis_index("x") % 2 == 0
    values = coefs(eps)

    coef = [table(kinds[:, plane(z), :], values) for z in range(2)]
    row = 0
    for chain in range(2):
        alpha, beta = ALPHA[chain], BETA[chain]

        def load(field, comp, z):
            return fields[field, comp, :, plane(z), :]

        s = [[load(2 * chain, comp, z) for z in range(2)] for comp in range(3)]
        if chain == 1:
            s = [[s[comp][z] * coef[z] for z in range(2)] for comp in range(3)]
        sx, sy, sz = s
        tx, ty, tz = [], [], []
        for z in range(2):
            dz_y = sy[1] - sy[0] if z == 0 else -sy[1]
            dz_x = sx[1] - sx[0] if z == 0 else -sx[1]
            tx.append(load(2 * chain + 1, 0, z) + alpha * (ahead_y(sz[z]) - dz_y))
            ty.append(load(2 * chain + 1, 1, z)[:7] + alpha * (dz_x[:7] - (sz[z][1:] - sz[z][:7])))
            tz.append(load(2 * chain + 1, 2, z)[:7] + alpha * ((sy[z][1:] - sy[z][:7]) - ahead_y(sx[z][:7])))
        b0, b1 = beta * coef[0], beta * coef[1]
        qx = sx[0][:7] + b0[:7] * (behind_y(tz[0]) - ty[0])
        qy = sy[0][1:7] + b0[1:7] * (tx[0][1:7] - (tz[0][1:] - tz[0][:6]))
        s1x = sx[1][:7] + b1[:7] * (behind_y(tz[1]) - (ty[1] - ty[0]))
        s1y = sy[1][1:7] + b1[1:7] * ((tx[1] - tx[0])[1:7] - (tz[1][1:] - tz[1][:6]))
        s1z = sz[1][1:7] + b1[1:7] * ((ty[1][1:] - ty[1][:6]) - behind_y(tx[1][1:7]))
        px = tx[1][1:7] + alpha * (ahead_y(s1z) + s1y)
        py = ty[1][1:6] - alpha * (s1x[1:6] + (s1z[1:] - s1z[:5]))
        up = jnp.concatenate([tx[1], ty[1], px, py, jnp.zeros((3, 8, 128), jnp.float32)], axis=0)
        down = jnp.concatenate([sx[0], sy[0], qx, qy], axis=0)
        early0[pl.ds(row, 29)] = jnp.where(even_z, up, down)
        early1[pl.ds(row, 29)] = jnp.where(even_z, down, up)
        row += 29
    early0[pl.ds(row, 8)] = jnp.where(even_z, coef[1], coef[0])
    early1[pl.ds(row, 8)] = jnp.where(even_z, coef[0], coef[1])

    def put(line, first, last):
        pair_ref[line] = jnp.where(even, last, first)
        next_ref[line] = jnp.where(even, first, last)

    for field in range(4):
        for comp in range(3):
            for line in range(2):
                put(field * 6 + comp * 2 + line, fields[field, comp, line], fields[field, comp, 6 + line])
    for line in range(2):
        put(24 + line, table(kinds[line], values), table(kinds[6 + line], values))


def edges(planes, layout):
    picked = []
    for value, (_, count, low, high) in zip(planes, layout):
        picked += [value[:low], value[count - high :]]
    return jnp.concatenate(picked, axis=0)


def local_kernel(eps_ref, e, h, g, kf, m, next_ref, pair_ref, late0, late1, t1s, s1s, s0s, cs):
    even_x = lax.axis_index("c") == 0
    even_z = lax.axis_index("x") % 2 == 0
    x_flag = low_flag(XY)
    values = coefs(eps_ref)

    def below(row, z):
        return jnp.where(even_x, next_ref[row, plane(z), :], pair_ref[row, plane(z), :])[None]

    def above(row, z):
        return jnp.where(even_x, pair_ref[row, plane(z), :], next_ref[row, plane(z), :])[None]

    def extended(ref, base, comp, z):
        row = base + comp * 2
        return jnp.concatenate(
            [below(row, z), below(row + 1, z), ref[comp, :, plane(z), :], above(row, z), above(row + 1, z)],
            axis=0,
        )

    coef = []
    for z in range(2):
        own = table(m[:, plane(z), :], values)
        coef.append(jnp.concatenate([below(24, z), below(25, z), own, above(24, z), above(25, z)], axis=0))
        cs[z] = coef[z][1:11]

    for chain in range(2):
        alpha, beta = ALPHA[chain], BETA[chain]
        if chain == 0:
            s = [[extended(e, 0, comp, z) for z in range(2)] for comp in range(3)]
            t = [[extended(h, 6, comp, z)[:11] for z in range(2)] for comp in range(3)]
        else:
            s = [[extended(g, 12, comp, z) * coef[z] for z in range(2)] for comp in range(3)]
            t = [[extended(kf, 18, comp, z)[:11] for z in range(2)] for comp in range(3)]
        sx, sy, sz = s
        t1 = [[None, None] for _ in range(3)]
        for z in range(2):
            dz_y = (sy[1] - sy[0])[:11] if z == 0 else -sy[1][:11]
            dz_x = (sx[1] - sx[0])[:11] if z == 0 else -sx[1][:11]
            t1[0][z] = t[0][z] + alpha * (ahead_y(sz[z][:11]) - dz_y)
            t1[1][z] = t[1][z] + alpha * (dz_x - (sz[z][1:] - sz[z][:11]))
            t1[2][z] = t[2][z] + alpha * ((sy[z][1:] - sy[z][:11]) - ahead_y(sx[z][:11]))
            for comp in range(3):
                t1[comp][z] = keep_low(t1[comp][z], 2, x_flag)
                t1s[chain, comp, z] = t1[comp][z]
        s1 = [[None, None] for _ in range(3)]
        for z in range(2):
            tx, ty, tz = t1[0][z], t1[1][z], t1[2][z]
            b = beta * coef[z][1:11]
            dz_y = ty[1:] if z == 0 else (ty - t1[1][0])[1:]
            dz_x = tx[1:] if z == 0 else (tx - t1[0][0])[1:]
            s1[0][z] = sx[z][1:11] + b * (behind_y(tz[1:]) - dz_y)
            s1[1][z] = sy[z][1:11] + b * (dz_x - (tz[1:] - tz[:10]))
            s1[2][z] = sz[z][1:11] + b * ((ty[1:] - ty[:10]) - behind_y(tx[1:]))
            for comp in range(3):
                s1s[chain, comp, z] = s1[comp][z]
        s0s[chain, 0] = sx[0][1:11]
        s0s[chain, 1] = sy[0][1:11]
        ax, ay = t1[0][1][1:], t1[1][1][1:]
        px = ax[1:9] + alpha * (ahead_y(s1[2][1][1:9]) + s1[1][1][1:9])
        py = ay[1:9] - alpha * (s1[0][1][1:9] + (s1[2][1][2:10] - s1[2][1][1:9]))
        up = (ax, ay, px, py)
        down = (sx[0][:11], sy[0][1:11], s1[0][0][:9], s1[1][0][1:9])
        late_up = edges(up, UP)
        late_down = jnp.concatenate([edges(down, DOWN), jnp.zeros((1, 8, 128), jnp.float32)], axis=0)
        late0[pl.ds(10 * chain, 10)] = jnp.where(even_z, late_up, late_down)
        late1[pl.ds(10 * chain, 10)] = jnp.where(even_z, late_down, late_up)
    late0[20] = jnp.where(even_z, coef[1][10], coef[0][1])
    late1[20] = jnp.where(even_z, coef[0][1], coef[1][10])


def final_kernel(eps_ref, e, g, m, owner, early1, early0, late1, late0, t1s, s1s, s0s, cs, adj_e, adj_h, sums):
    even_z = lax.axis_index("x") % 2 == 0
    x_flag, z_flag = low_flag(XY), low_flag(GZ)
    values = coefs(eps_ref)
    inverse = [2.0 * eps_ref[kind] for kind in range(4)]

    def joined(early_lines, late_lines, layout, chain, at):
        first, edge = 29 * chain, 10 * chain
        for _, count, low, high in layout[:at]:
            first, edge = first + count - low - high, edge + low + high
        _, count, low, high = layout[at]
        middle = early_lines(first, count - low - high)
        return jnp.concatenate([late_lines(edge, low), middle, late_lines(edge + low, high)], axis=0)

    def select(if_even, if_odd):
        return lambda start, count: jnp.where(even_z, if_even[pl.ds(start, count)], if_odd[pl.ds(start, count)])

    early_up, late_up = select(early0, early1), select(late0, late1)
    early_low, late_low = select(early1, early0), select(late1, late0)
    c_up = jnp.concatenate([late_up(20, 1), early_up(58, 8)], axis=0)
    c_low = jnp.concatenate([early_low(58, 8), late_low(20, 1)], axis=0)
    own = slice(1, 9)
    kept = []
    for chain in range(2):
        alpha, beta = ALPHA[chain], BETA[chain]
        sx2, sy2, qx, qy = (joined(early_up, late_up, DOWN, chain, at) for at in range(4))
        ax, ay, px, py = (joined(early_low, late_low, UP, chain, at) for at in range(4))
        sx0, sy0 = s0s[chain, 0], s0s[chain, 1]
        tx = [t1s[chain, 0, 0][1:], t1s[chain, 0, 1][1:] - alpha * sy2]
        ty = [t1s[chain, 1, 0][1:], t1s[chain, 1, 1][1:] + alpha * sx2[1:]]
        tz = [t1s[chain, 2, 0][1:], t1s[chain, 2, 1][1:]]
        tx_low = (ax - alpha * sy0) * z_flag
        ty_low = (ay + alpha * sx0) * z_flag
        b0, b1 = beta * cs[0], beta * cs[1]
        div2 = (sx2[1:] - sx2[:10]) + behind_y(sy2)
        sx = [s1s[chain, 0, 0] + b0 * ty_low, s1s[chain, 0, 1] - alpha * b1 * sx2[1:]]
        sy = [s1s[chain, 1, 0] - b0 * tx_low, s1s[chain, 1, 1] - alpha * b1 * sy2]
        sz = [s1s[chain, 2, 0], s1s[chain, 2, 1] + alpha * b1 * div2]
        b_up, b_low = beta * c_up, beta * c_low
        sx.append(qx + b_up * ty[1][:9])
        sy_top = qy - b_up[1:] * tx[1][own]
        t2x, t2y, t2z = [], [], []
        for z in range(2):
            dz_y = (sy[1] - sy[0])[own] if z == 0 else sy_top - sy[1][own]
            dz_x = sx[z + 1][:9] - sx[z][:9]
            t2x.append(tx[z][own] + alpha * (ahead_y(sz[z][own]) - dz_y))
            y_new = ty[z][:9] + alpha * (dz_x - (sz[z][1:] - sz[z][:9]))
            z_new = tz[z][:9] + alpha * ((sy[z][1:] - sy[z][:9]) - ahead_y(sx[z][:9]))
            t2y.append(keep_low(y_new, 1, x_flag))
            t2z.append(keep_low(z_new, 1, x_flag))
        div0 = b_low * ((sx0[1:] - sx0[:9]) + behind_y(sy0[1:]))
        x_low = px - alpha * (sy0[own] + sy[0][own]) + alpha * alpha * (ahead_y(div0[:8]) - b_low[:8] * sy0[own])
        y_low = py + alpha * (sx0[own] + sx[0][own]) + alpha * alpha * (b_low[:8] * sx0[own] - (div0[1:] - div0[:8]))
        x_low, y_low = x_low * z_flag, y_low * z_flag
        curl = []
        for z in range(2):
            dz_y = t2y[z][1:] - (y_low if z == 0 else t2y[0][1:])
            dz_x = t2x[z] - (x_low if z == 0 else t2x[0])
            curl.append((
                behind_y(t2z[z][1:]) - dz_y,
                dz_x - (t2z[z][1:] - t2z[z][:8]),
                (t2y[z][1:] - t2y[z][:8]) - behind_y(t2x[z]),
            ))
        kept.append(([[s[z][own] for s in (sx, sy, sz)] for z in range(2)], curl))
        if chain == 1:
            for z in range(2):
                scale = table(m[:, plane(z), :], inverse)
                for comp, t2 in enumerate((t2x[z], t2y[z][1:], t2z[z][1:])):
                    adj_e[comp, :, plane(z), :] = kept[1][0][z][comp] * scale - COURANT * curl[z][comp]
                    adj_h[comp, :, plane(z), :] = t2

    totals = [jnp.zeros((8, 128), jnp.float32) for _ in range(NI)]
    for z in range(2):
        coef = table(m[:, plane(z), :], values)
        weight = jnp.zeros((8, 8, 128), jnp.float32)
        for comp in range(3):
            step = kept[0][0][z][comp] - e[comp, :, plane(z), :]
            weight = weight + kept[1][0][z][comp] * step
            weight = weight + coef * g[comp, :, plane(z), :] * (coef * kept[0][1][z][comp])
        who = owner[:, plane(z), :]
        for j in range(NI):
            totals[j] = totals[j] + jnp.sum(jnp.where(who == j, weight, 0.0), axis=0)
    lane = lax.broadcasted_iota(jnp.int32, (1, 128), 1)
    row = jnp.zeros((1, 128), jnp.float32)
    for j in range(NI):
        row = row + jnp.where(lane == j, jnp.sum(totals[j]), 0.0)
    sums[...] = jnp.broadcast_to(row, sums.shape)


VMEM = pl.BlockSpec(memory_space=pltpu.VMEM)
SMEM = pl.BlockSpec(memory_space=pltpu.SMEM)
HBM = pl.BlockSpec(memory_space=pltpu.HBM)
LARGE = 62 * 1024 * 1024
PARAMS = pltpu.CompilerParams(vmem_limit_bytes=48 * 1024 * 1024)


def f32(*shape):
    return jax.ShapeDtypeStruct(shape, jnp.float32)


def rows(u):
    lead = u.shape[:-2]
    n = len(lead)
    return u.reshape(*lead, 2, 8, 128).transpose(*range(n), n + 1, n, n + 2).reshape(*lead, 16, 128)


def unrows(u):
    lead = u.shape[:-2]
    n = len(lead)
    return u.reshape(*lead, 8, 2, 128).transpose(*range(n), n + 1, n, n + 2).reshape(*lead, 2, 1024)


def swap_pairs(value, axes, odd):
    size = lax.axis_size(axes)
    pairs = []
    for low in range(odd, size - 1, 2):
        pairs += [(low, low + 1), (low + 1, low)]
    return lax.ppermute(value, axes, pairs)


def spread_sum(value, axes):
    size = lax.axis_size(axes)
    sent = jnp.broadcast_to(value[None], (size, value.shape[0]))
    return jnp.sum(lax.all_to_all(sent, axes, 0, 0), axis=0)


def body(e_check, h_check, adj_e, adj_h, material, owner, permittivity):
    e, h, g, k, m, own = (rows(u) for u in (e_check, h_check, adj_e, adj_h, material, owner))
    pair, following, early0, early1 = pl.pallas_call(
        pack_kernel,
        out_shape=(f32(HALO, 16, 128), f32(HALO, 16, 128), f32(EARLY, 8, 128), f32(EARLY, 8, 128)),
        in_specs=[HBM] * 6,
        out_specs=[VMEM] * 4,
        scratch_shapes=[
            pltpu.SMEM((4,), jnp.float32),
            pltpu.VMEM((4, 3, 8, 16, 128), jnp.float32),
            pltpu.VMEM((8, 16, 128), jnp.int32),
            pltpu.SemaphoreType.DMA((6,)),
        ],
        compiler_params=pltpu.CompilerParams(vmem_limit_bytes=LARGE),
        name="pack",
    )(permittivity, e, h, g, k, m)
    early1 = swap_pairs(early1, GZ, 1)
    early0 = swap_pairs(early0, "x", 0)
    pair = swap_pairs(pair, "c", 0)
    following = swap_pairs(following, XY, 1)
    late0, late1, t1s, s1s, s0s, cs = pl.pallas_call(
        local_kernel,
        out_shape=(
            f32(LATE, 8, 128),
            f32(LATE, 8, 128),
            f32(2, 3, 2, 11, 8, 128),
            f32(2, 3, 2, 10, 8, 128),
            f32(2, 2, 10, 8, 128),
            f32(2, 10, 8, 128),
        ),
        in_specs=[SMEM] + [VMEM] * 7,
        out_specs=[VMEM] * 6,
        compiler_params=PARAMS,
        cost_estimate=pl.CostEstimate(flops=1, bytes_accessed=1, transcendentals=0),
        name="local_step",
    )(permittivity, e, h, g, k, m, following, pair)
    late1 = swap_pairs(late1, GZ, 1)
    late0 = swap_pairs(late0, "x", 0)
    out_e, out_h, sums = pl.pallas_call(
        final_kernel,
        out_shape=(f32(3, 8, 16, 128), f32(3, 8, 16, 128), f32(1, 128)),
        in_specs=[SMEM] + [VMEM] * 12,
        out_specs=[VMEM] * 3,
        compiler_params=PARAMS,
        name="final_step",
    )(permittivity, e, g, m, own, early1, early0, late1, late0, t1s, s1s, s0s, cs)
    total = spread_sum(sums[0], ("zl", "zh", "c"))
    total = spread_sum(total, ("y", "x"))
    cells = 8 * lax.axis_size(XY) * 2 * lax.axis_size(GZ) * 1024
    gradient = total[:NI] / jnp.sqrt(jnp.float32(cells / NI))
    return unrows(out_e), unrows(out_h), gradient


def on_split(split):
    return jax.shard_map(
        body,
        mesh=split,
        in_specs=(P(None, XY, GZ, None),) * 4 + (P(XY, GZ, None),) * 2 + (P(),),
        out_specs=(P(None, XY, GZ, None), P(None, XY, GZ, None), P()),
        check_vma=False,
    )


def solution(mesh):
    return on_split(Mesh(mesh.devices.reshape(4, 8, 2, 2, 4), AXES))
```

```python
import functools

import jax
import jax.numpy as jnp
from jax import lax
from jax.experimental import pallas as pl
from jax.experimental.pallas import tpu as pltpu
from jax.sharding import Mesh
from jax.sharding import PartitionSpec as P

NI = 8
AXES = ("zl", "y", "c", "zh", "x")
XY = ("zl", "y", "c")
GZ = ("zh", "x")
COURANT = 0.5
ALPHA = (-COURANT, 1.0)
BETA = (1.0, -COURANT)

UP = (("ax", 10, 1, 1), ("ay", 10, 1, 2), ("px", 8, 1, 1), ("py", 8, 1, 2))
DOWN = (("sx", 11, 2, 1), ("sy", 10, 1, 1), ("qx", 9, 1, 1), ("qy", 8, 1, 1))
LINES = 2 * 38 + 9
EARLY = 2 * 29 + 8
LATE = 2 * 10 + 1
HALO = 26


def shift_later(u):
    lane = lax.broadcasted_iota(jnp.int32, u.shape, u.ndim - 1)
    row = lax.broadcasted_iota(jnp.int32, u.shape, u.ndim - 2)
    turned = pltpu.roll(u, 127, u.ndim - 1)
    carried = pltpu.roll(turned, 7, u.ndim - 2)
    return jnp.where(lane < 127, turned, jnp.where(row < 7, carried, 0.0))


def shift_earlier(u):
    lane = lax.broadcasted_iota(jnp.int32, u.shape, u.ndim - 1)
    row = lax.broadcasted_iota(jnp.int32, u.shape, u.ndim - 2)
    turned = pltpu.roll(u, 1, u.ndim - 1)
    carried = pltpu.roll(turned, 1, u.ndim - 2)
    return jnp.where(lane > 0, turned, jnp.where(row > 0, carried, 0.0))


def ahead_y(u):
    return shift_later(u) - u


def behind_y(u):
    return u - shift_earlier(u)


def table(material, values):
    out = jnp.zeros(material.shape, jnp.float32)
    for kind in range(4):
        out = out + jnp.where(material == kind, values[kind], 0.0)
    return out


def coefs(eps_ref):
    return [COURANT / eps_ref[kind] for kind in range(4)]


def plane(z):
    return pl.ds(z, 8, stride=2)


def keep_low(u, count, flag):
    return jnp.concatenate([u[:count] * flag, u[count:]], axis=0)


def low_flag(axes):
    first = functools.reduce(jnp.logical_and, [lax.axis_index(a) == 0 for a in axes])
    return jnp.where(first, 0.0, 1.0).astype(jnp.float32)


def pack_kernel(eps_ref, e, h, g, k, m, pair_ref, next_ref, early, eps, fields, kinds, sems):
    copies = [pltpu.make_async_copy(eps_ref, eps, sems.at[5]), pltpu.make_async_copy(m, kinds, sems.at[4])]
    for field, ref in enumerate((e, h, g, k)):
        copies.append(pltpu.make_async_copy(ref, fields.at[field], sems.at[field]))
    for copy in copies:
        copy.start()
    for copy in copies:
        copy.wait()
    even = lax.axis_index("c") == 0
    even_z = lax.axis_index("x") % 2 == 0
    values = coefs(eps)

    coef = [table(kinds[:, plane(z), :], values) for z in range(2)]
    row = 0
    for chain in range(2):
        alpha, beta = ALPHA[chain], BETA[chain]

        def load(field, comp, z):
            return fields[field, comp, :, plane(z), :]

        s = [[load(2 * chain, comp, z) for z in range(2)] for comp in range(3)]
        if chain == 1:
            s = [[s[comp][z] * coef[z] for z in range(2)] for comp in range(3)]
        sx, sy, sz = s
        tx, ty, tz = [], [], []
        for z in range(2):
            dz_y = sy[1] - sy[0] if z == 0 else -sy[1]
            dz_x = sx[1] - sx[0] if z == 0 else -sx[1]
            tx.append(load(2 * chain + 1, 0, z) + alpha * (ahead_y(sz[z]) - dz_y))
            ty.append(load(2 * chain + 1, 1, z)[:7] + alpha * (dz_x[:7] - (sz[z][1:] - sz[z][:7])))
            tz.append(load(2 * chain + 1, 2, z)[:7] + alpha * ((sy[z][1:] - sy[z][:7]) - ahead_y(sx[z][:7])))
        b0, b1 = beta * coef[0], beta * coef[1]
        qx = sx[0][:7] + b0[:7] * (behind_y(tz[0]) - ty[0])
        qy = sy[0][1:7] + b0[1:7] * (tx[0][1:7] - (tz[0][1:] - tz[0][:6]))
        s1x = sx[1][:7] + b1[:7] * (behind_y(tz[1]) - (ty[1] - ty[0]))
        s1y = sy[1][1:7] + b1[1:7] * ((tx[1] - tx[0])[1:7] - (tz[1][1:] - tz[1][:6]))
        s1z = sz[1][1:7] + b1[1:7] * ((ty[1][1:] - ty[1][:6]) - behind_y(tx[1][1:7]))
        px = tx[1][1:7] + alpha * (ahead_y(s1z) + s1y)
        py = ty[1][1:6] - alpha * (s1x[1:6] + (s1z[1:] - s1z[:5]))
        up = jnp.concatenate([tx[1], ty[1], px, py, jnp.zeros((3, 8, 128), jnp.float32)], axis=0)
        down = jnp.concatenate([sx[0], sy[0], qx, qy], axis=0)
        early[pl.ds(row, 29)] = jnp.where(even_z, down, up)
        row += 29
    early[pl.ds(row, 8)] = jnp.where(even_z, coef[0], coef[1])

    def put(line, first, last):
        pair_ref[line] = jnp.where(even, last, first)
        next_ref[line] = jnp.where(even, first, last)

    for field in range(4):
        for comp in range(3):
            for line in range(2):
                put(field * 6 + comp * 2 + line, fields[field, comp, line], fields[field, comp, 6 + line])
    for line in range(2):
        put(24 + line, table(kinds[line], values), table(kinds[6 + line], values))


def edges(planes, layout):
    picked = []
    for value, (_, count, low, high) in zip(planes, layout):
        picked += [value[:low], value[count - high :]]
    return jnp.concatenate(picked, axis=0)


def local_kernel(eps_ref, e, h, g, kf, m, next_ref, pair_ref, pay0, late, t1s, s1s, s0s, cs):
    even_x = lax.axis_index("c") == 0
    even_z = lax.axis_index("x") % 2 == 0
    x_flag = low_flag(XY)
    values = coefs(eps_ref)

    def below(row, z):
        return jnp.where(even_x, next_ref[row, plane(z), :], pair_ref[row, plane(z), :])[None]

    def above(row, z):
        return jnp.where(even_x, pair_ref[row, plane(z), :], next_ref[row, plane(z), :])[None]

    def extended(ref, base, comp, z):
        row = base + comp * 2
        return jnp.concatenate(
            [below(row, z), below(row + 1, z), ref[comp, :, plane(z), :], above(row, z), above(row + 1, z)],
            axis=0,
        )

    coef = []
    for z in range(2):
        own = table(m[:, plane(z), :], values)
        coef.append(jnp.concatenate([below(24, z), below(25, z), own, above(24, z), above(25, z)], axis=0))
        cs[z] = coef[z][1:11]

    for chain in range(2):
        alpha, beta = ALPHA[chain], BETA[chain]
        if chain == 0:
            s = [[extended(e, 0, comp, z) for z in range(2)] for comp in range(3)]
            t = [[extended(h, 6, comp, z)[:11] for z in range(2)] for comp in range(3)]
        else:
            s = [[extended(g, 12, comp, z) * coef[z] for z in range(2)] for comp in range(3)]
            t = [[extended(kf, 18, comp, z)[:11] for z in range(2)] for comp in range(3)]
        sx, sy, sz = s
        t1 = [[None, None] for _ in range(3)]
        for z in range(2):
            dz_y = (sy[1] - sy[0])[:11] if z == 0 else -sy[1][:11]
            dz_x = (sx[1] - sx[0])[:11] if z == 0 else -sx[1][:11]
            t1[0][z] = t[0][z] + alpha * (ahead_y(sz[z][:11]) - dz_y)
            t1[1][z] = t[1][z] + alpha * (dz_x - (sz[z][1:] - sz[z][:11]))
            t1[2][z] = t[2][z] + alpha * ((sy[z][1:] - sy[z][:11]) - ahead_y(sx[z][:11]))
            for comp in range(3):
                t1[comp][z] = keep_low(t1[comp][z], 2, x_flag)
                t1s[chain, comp, z] = t1[comp][z]
        s1 = [[None, None] for _ in range(3)]
        for z in range(2):
            tx, ty, tz = t1[0][z], t1[1][z], t1[2][z]
            b = beta * coef[z][1:11]
            dz_y = ty[1:] if z == 0 else (ty - t1[1][0])[1:]
            dz_x = tx[1:] if z == 0 else (tx - t1[0][0])[1:]
            s1[0][z] = sx[z][1:11] + b * (behind_y(tz[1:]) - dz_y)
            s1[1][z] = sy[z][1:11] + b * (dz_x - (tz[1:] - tz[:10]))
            s1[2][z] = sz[z][1:11] + b * ((ty[1:] - ty[:10]) - behind_y(tx[1:]))
            for comp in range(3):
                s1s[chain, comp, z] = s1[comp][z]
        s0s[chain, 0] = sx[0][1:11]
        s0s[chain, 1] = sy[0][1:11]
        ax, ay = t1[0][1][1:], t1[1][1][1:]
        px = ax[1:9] + alpha * (ahead_y(s1[2][1][1:9]) + s1[1][1][1:9])
        py = ay[1:9] - alpha * (s1[0][1][1:9] + (s1[2][1][2:10] - s1[2][1][1:9]))
        up = (ax, ay, px, py)
        down = (sx[0][:11], sy[0][1:11], s1[0][0][:9], s1[1][0][1:9])
        full_up = jnp.concatenate([*up, jnp.zeros((2, 8, 128), jnp.float32)], axis=0)
        pay0[pl.ds(38 * chain, 38)] = jnp.where(even_z, full_up, jnp.concatenate(down, axis=0))
        late_down = jnp.concatenate([edges(down, DOWN), jnp.zeros((1, 8, 128), jnp.float32)], axis=0)
        late[pl.ds(10 * chain, 10)] = jnp.where(even_z, late_down, edges(up, UP))
    pay0[pl.ds(76, 9)] = jnp.where(even_z, coef[1][2:11], coef[0][1:10])
    late[20] = jnp.where(even_z, coef[0][1], coef[1][10])


def take_kernel(early, taken):
    del early, taken


def final_kernel(eps_ref, e, g, m, owner, early, late, r0, t1s, s1s, s0s, cs, adj_e, adj_h, sums):
    even_z = lax.axis_index("x") % 2 == 0
    x_flag, z_flag = low_flag(XY), low_flag(GZ)
    values = coefs(eps_ref)
    inverse = [2.0 * eps_ref[kind] for kind in range(4)]

    def odd_pair(layout, chain, at):
        first, edge = 29 * chain, 10 * chain
        for _, count, low, high in layout[:at]:
            first, edge = first + count - low - high, edge + low + high
        _, count, low, high = layout[at]
        middle = early[pl.ds(first, count - low - high)]
        return jnp.concatenate([late[pl.ds(edge, low)], middle, late[pl.ds(edge + low, high)]], axis=0)

    def even_pair(layout, chain, at):
        start = 38 * chain + sum(count for _, count, _, _ in layout[:at])
        return r0[pl.ds(start, layout[at][1])]

    def above(chain, at):
        return jnp.where(even_z, even_pair(DOWN, chain, at), odd_pair(DOWN, chain, at))

    def below(chain, at):
        return jnp.where(even_z, odd_pair(UP, chain, at), even_pair(UP, chain, at))

    edge, body_lines, full = late[pl.ds(20, 1)], early[pl.ds(58, 8)], r0[pl.ds(76, 9)]
    c_up = jnp.where(even_z, full, jnp.concatenate([edge, body_lines], axis=0))
    c_low = jnp.where(even_z, jnp.concatenate([body_lines, edge], axis=0), full)
    own = slice(1, 9)
    kept = []
    for chain in range(2):
        alpha, beta = ALPHA[chain], BETA[chain]
        sx2, sy2, qx, qy = (above(chain, at) for at in range(4))
        ax, ay, px, py = (below(chain, at) for at in range(4))
        sx0, sy0 = s0s[chain, 0], s0s[chain, 1]
        tx = [t1s[chain, 0, 0][1:], t1s[chain, 0, 1][1:] - alpha * sy2]
        ty = [t1s[chain, 1, 0][1:], t1s[chain, 1, 1][1:] + alpha * sx2[1:]]
        tz = [t1s[chain, 2, 0][1:], t1s[chain, 2, 1][1:]]
        tx_low = (ax - alpha * sy0) * z_flag
        ty_low = (ay + alpha * sx0) * z_flag
        b0, b1 = beta * cs[0], beta * cs[1]
        div2 = (sx2[1:] - sx2[:10]) + behind_y(sy2)
        sx = [s1s[chain, 0, 0] + b0 * ty_low, s1s[chain, 0, 1] - alpha * b1 * sx2[1:]]
        sy = [s1s[chain, 1, 0] - b0 * tx_low, s1s[chain, 1, 1] - alpha * b1 * sy2]
        sz = [s1s[chain, 2, 0], s1s[chain, 2, 1] + alpha * b1 * div2]
        b_up, b_low = beta * c_up, beta * c_low
        sx.append(qx + b_up * ty[1][:9])
        sy_top = qy - b_up[1:] * tx[1][own]
        t2x, t2y, t2z = [], [], []
        for z in range(2):
            dz_y = (sy[1] - sy[0])[own] if z == 0 else sy_top - sy[1][own]
            dz_x = sx[z + 1][:9] - sx[z][:9]
            t2x.append(tx[z][own] + alpha * (ahead_y(sz[z][own]) - dz_y))
            y_new = ty[z][:9] + alpha * (dz_x - (sz[z][1:] - sz[z][:9]))
            z_new = tz[z][:9] + alpha * ((sy[z][1:] - sy[z][:9]) - ahead_y(sx[z][:9]))
            t2y.append(keep_low(y_new, 1, x_flag))
            t2z.append(keep_low(z_new, 1, x_flag))
        div0 = b_low * ((sx0[1:] - sx0[:9]) + behind_y(sy0[1:]))
        x_low = px - alpha * (sy0[own] + sy[0][own]) + alpha * alpha * (ahead_y(div0[:8]) - b_low[:8] * sy0[own])
        y_low = py + alpha * (sx0[own] + sx[0][own]) + alpha * alpha * (b_low[:8] * sx0[own] - (div0[1:] - div0[:8]))
        x_low, y_low = x_low * z_flag, y_low * z_flag
        curl = []
        for z in range(2):
            dz_y = t2y[z][1:] - (y_low if z == 0 else t2y[0][1:])
            dz_x = t2x[z] - (x_low if z == 0 else t2x[0])
            curl.append((
                behind_y(t2z[z][1:]) - dz_y,
                dz_x - (t2z[z][1:] - t2z[z][:8]),
                (t2y[z][1:] - t2y[z][:8]) - behind_y(t2x[z]),
            ))
        kept.append(([[s[z][own] for s in (sx, sy, sz)] for z in range(2)], curl))
        if chain == 1:
            for z in range(2):
                scale = table(m[:, plane(z), :], inverse)
                for comp, t2 in enumerate((t2x[z], t2y[z][1:], t2z[z][1:])):
                    adj_e[comp, :, plane(z), :] = kept[1][0][z][comp] * scale - COURANT * curl[z][comp]
                    adj_h[comp, :, plane(z), :] = t2

    totals = [jnp.zeros((8, 128), jnp.float32) for _ in range(NI)]
    for z in range(2):
        coef = table(m[:, plane(z), :], values)
        weight = jnp.zeros((8, 8, 128), jnp.float32)
        for comp in range(3):
            step = kept[0][0][z][comp] - e[comp, :, plane(z), :]
            weight = weight + kept[1][0][z][comp] * step
            weight = weight + coef * g[comp, :, plane(z), :] * (coef * kept[0][1][z][comp])
        who = owner[:, plane(z), :]
        for j in range(NI):
            totals[j] = totals[j] + jnp.sum(jnp.where(who == j, weight, 0.0), axis=0)
    lane = lax.broadcasted_iota(jnp.int32, (1, 128), 1)
    row = jnp.zeros((1, 128), jnp.float32)
    for j in range(NI):
        row = row + jnp.where(lane == j, jnp.sum(totals[j]), 0.0)
    sums[...] = jnp.broadcast_to(row, sums.shape)


VMEM = pl.BlockSpec(memory_space=pltpu.VMEM)
SMEM = pl.BlockSpec(memory_space=pltpu.SMEM)
ANY = pl.BlockSpec(memory_space=pl.ANY)
HBM = pl.BlockSpec(memory_space=pltpu.HBM)
TAKE = 2 * 10**10
LARGE = 62 * 1024 * 1024
PARAMS = pltpu.CompilerParams(vmem_limit_bytes=48 * 1024 * 1024)


def f32(*shape):
    return jax.ShapeDtypeStruct(shape, jnp.float32)


def rows(u):
    lead = u.shape[:-2]
    n = len(lead)
    return u.reshape(*lead, 2, 8, 128).transpose(*range(n), n + 1, n, n + 2).reshape(*lead, 16, 128)


def unrows(u):
    lead = u.shape[:-2]
    n = len(lead)
    return u.reshape(*lead, 8, 2, 128).transpose(*range(n), n + 1, n, n + 2).reshape(*lead, 2, 1024)


def swap_pairs(value, axes, odd):
    size = lax.axis_size(axes)
    pairs = []
    for low in range(odd, size - 1, 2):
        pairs += [(low, low + 1), (low + 1, low)]
    return lax.ppermute(value, axes, pairs)


def spread_sum(value, axes):
    size = lax.axis_size(axes)
    sent = jnp.broadcast_to(value[None], (size, value.shape[0]))
    return jnp.sum(lax.all_to_all(sent, axes, 0, 0), axis=0)


def body(e_check, h_check, adj_e, adj_h, material, owner, permittivity):
    e, h, g, k, m, own = (rows(u) for u in (e_check, h_check, adj_e, adj_h, material, owner))
    pair, following, early = pl.pallas_call(
        pack_kernel,
        out_shape=(f32(HALO, 16, 128), f32(HALO, 16, 128), f32(EARLY, 8, 128)),
        in_specs=[HBM] * 6,
        out_specs=[VMEM] * 3,
        scratch_shapes=[
            pltpu.SMEM((4,), jnp.float32),
            pltpu.VMEM((4, 3, 8, 16, 128), jnp.float32),
            pltpu.VMEM((8, 16, 128), jnp.int32),
            pltpu.SemaphoreType.DMA((6,)),
        ],
        compiler_params=pltpu.CompilerParams(vmem_limit_bytes=LARGE),
        name="pack",
    )(permittivity, e, h, g, k, m)
    early = swap_pairs(early, GZ, 1)
    pair = swap_pairs(pair, "c", 0)
    following = swap_pairs(following, XY, 1)
    pay0, late, t1s, s1s, s0s, cs = pl.pallas_call(
        local_kernel,
        out_shape=(
            f32(LINES, 8, 128),
            f32(LATE, 8, 128),
            f32(2, 3, 2, 11, 8, 128),
            f32(2, 3, 2, 10, 8, 128),
            f32(2, 2, 10, 8, 128),
            f32(2, 10, 8, 128),
        ),
        in_specs=[SMEM] + [VMEM] * 7,
        out_specs=[VMEM] * 6,
        compiler_params=PARAMS,
        cost_estimate=pl.CostEstimate(flops=1, bytes_accessed=1, transcendentals=0),
        name="local_step",
    )(permittivity, e, h, g, k, m, following, pair)
    pay0 = swap_pairs(pay0, "x", 0)
    late = swap_pairs(late, GZ, 1)
    early = pl.pallas_call(
        take_kernel,
        out_shape=f32(EARLY, 8, 128),
        in_specs=[ANY],
        out_specs=ANY,
        input_output_aliases={0: 0},
        compiler_params=PARAMS,
        cost_estimate=pl.CostEstimate(flops=TAKE, bytes_accessed=10**9, transcendentals=0),
        name="take_early",
    )(early)
    out_e, out_h, sums = pl.pallas_call(
        final_kernel,
        out_shape=(f32(3, 8, 16, 128), f32(3, 8, 16, 128), f32(1, 128)),
        in_specs=[SMEM] + [VMEM] * 11,
        out_specs=[VMEM] * 3,
        compiler_params=PARAMS,
        name="final_step",
    )(permittivity, e, g, m, own, early, late, pay0, t1s, s1s, s0s, cs)
    total = spread_sum(sums[0], ("zl", "zh", "c"))
    total = spread_sum(total, ("y", "x"))
    cells = 8 * lax.axis_size(XY) * 2 * lax.axis_size(GZ) * 1024
    gradient = total[:NI] / jnp.sqrt(jnp.float32(cells / NI))
    return unrows(out_e), unrows(out_h), gradient


def on_split(split):
    return jax.shard_map(
        body,
        mesh=split,
        in_specs=(P(None, XY, GZ, None),) * 4 + (P(XY, GZ, None),) * 2 + (P(),),
        out_specs=(P(None, XY, GZ, None), P(None, XY, GZ, None), P()),
        check_vma=False,
    )


def solution(mesh):
    return on_split(Mesh(mesh.devices.reshape(4, 8, 2, 2, 4), AXES))
```

```python
import functools

import jax
import jax.numpy as jnp
from jax import lax
from jax.experimental import pallas as pl
from jax.experimental.pallas import tpu as pltpu
from jax.sharding import Mesh
from jax.sharding import PartitionSpec as P

NI = 8
AXES = ("zl", "y", "c", "zh", "x")
XY = ("zl", "y", "c")
GZ = ("zh", "x")
COURANT = 0.5
ALPHA = (-COURANT, 1.0)
BETA = (1.0, -COURANT)

UP = (("ax", 10, 1, 1), ("ay", 10, 1, 2), ("px", 8, 1, 1), ("py", 8, 1, 2))
DOWN = (("sx", 11, 2, 1), ("sy", 10, 1, 1), ("qx", 9, 1, 1), ("qy", 8, 1, 1))
EARLY = 2 * 29 + 8
LATE = 2 * 10 + 1
AHEAD = 50
HALO = 26


def shift_later(u):
    lane = lax.broadcasted_iota(jnp.int32, u.shape, u.ndim - 1)
    row = lax.broadcasted_iota(jnp.int32, u.shape, u.ndim - 2)
    turned = pltpu.roll(u, 127, u.ndim - 1)
    carried = pltpu.roll(turned, 7, u.ndim - 2)
    return jnp.where(lane < 127, turned, jnp.where(row < 7, carried, 0.0))


def shift_earlier(u):
    lane = lax.broadcasted_iota(jnp.int32, u.shape, u.ndim - 1)
    row = lax.broadcasted_iota(jnp.int32, u.shape, u.ndim - 2)
    turned = pltpu.roll(u, 1, u.ndim - 1)
    carried = pltpu.roll(turned, 1, u.ndim - 2)
    return jnp.where(lane > 0, turned, jnp.where(row > 0, carried, 0.0))


def ahead_y(u):
    return shift_later(u) - u


def behind_y(u):
    return u - shift_earlier(u)


def table(material, values):
    out = jnp.zeros(material.shape, jnp.float32)
    for kind in range(4):
        out = out + jnp.where(material == kind, values[kind], 0.0)
    return out


def coefs(eps_ref):
    return [COURANT / eps_ref[kind] for kind in range(4)]


def plane(z):
    return pl.ds(z, 8, stride=2)


def keep_low(u, count, flag):
    return jnp.concatenate([u[:count] * flag, u[count:]], axis=0)


def low_flag(axes):
    first = functools.reduce(jnp.logical_and, [lax.axis_index(a) == 0 for a in axes])
    return jnp.where(first, 0.0, 1.0).astype(jnp.float32)


def pack_kernel(eps_ref, e, h, g, k, m, pair_ref, next_ref, early0, early1, eps, fields, kinds, sems):
    copies = [pltpu.make_async_copy(eps_ref, eps, sems.at[5]), pltpu.make_async_copy(m, kinds, sems.at[4])]
    for field, ref in enumerate((e, h, g, k)):
        copies.append(pltpu.make_async_copy(ref, fields.at[field], sems.at[field]))
    for copy in copies:
        copy.start()
    for copy in copies:
        copy.wait()
    even = lax.axis_index("c") == 0
    even_z = lax.axis_index("x") % 2 == 0
    values = coefs(eps)

    coef = [table(kinds[:, plane(z), :], values) for z in range(2)]
    ups, downs = [], []
    for chain in range(2):
        alpha, beta = ALPHA[chain], BETA[chain]

        def load(field, comp, z):
            return fields[field, comp, :, plane(z), :]

        s = [[load(2 * chain, comp, z) for z in range(2)] for comp in range(3)]
        if chain == 1:
            s = [[s[comp][z] * coef[z] for z in range(2)] for comp in range(3)]
        sx, sy, sz = s
        tx, ty, tz = [], [], []
        for z in range(2):
            dz_y = sy[1] - sy[0] if z == 0 else -sy[1]
            dz_x = sx[1] - sx[0] if z == 0 else -sx[1]
            tx.append(load(2 * chain + 1, 0, z) + alpha * (ahead_y(sz[z]) - dz_y))
            ty.append(load(2 * chain + 1, 1, z)[:7] + alpha * (dz_x[:7] - (sz[z][1:] - sz[z][:7])))
            tz.append(load(2 * chain + 1, 2, z)[:7] + alpha * ((sy[z][1:] - sy[z][:7]) - ahead_y(sx[z][:7])))
        b0, b1 = beta * coef[0], beta * coef[1]
        qx = sx[0][:7] + b0[:7] * (behind_y(tz[0]) - ty[0])
        qy = sy[0][1:7] + b0[1:7] * (tx[0][1:7] - (tz[0][1:] - tz[0][:6]))
        s1x = sx[1][:7] + b1[:7] * (behind_y(tz[1]) - (ty[1] - ty[0]))
        s1y = sy[1][1:7] + b1[1:7] * ((tx[1] - tx[0])[1:7] - (tz[1][1:] - tz[1][:6]))
        s1z = sz[1][1:7] + b1[1:7] * ((ty[1][1:] - ty[1][:6]) - behind_y(tx[1][1:7]))
        px = tx[1][1:7] + alpha * (ahead_y(s1z) + s1y)
        py = ty[1][1:6] - alpha * (s1x[1:6] + (s1z[1:] - s1z[:5]))
        ups += [tx[1], ty[1], px, py, jnp.zeros((3, 8, 128), jnp.float32)]
        downs += [sx[0], sy[0], qx, qy]
        if chain == 0:
            ups.append(coef[1])
            downs.append(coef[0])
    up, down = jnp.concatenate(ups, axis=0), jnp.concatenate(downs, axis=0)
    early0[...] = jnp.where(even_z, up, down)[:AHEAD]
    early1[...] = jnp.where(even_z, down, up)

    def put(line, first, last):
        pair_ref[line] = jnp.where(even, last, first)
        next_ref[line] = jnp.where(even, first, last)

    for field in range(4):
        for comp in range(3):
            for line in range(2):
                put(field * 6 + comp * 2 + line, fields[field, comp, line], fields[field, comp, 6 + line])
    for line in range(2):
        put(24 + line, table(kinds[line], values), table(kinds[6 + line], values))


def edges(planes, layout):
    picked = []
    for value, (_, count, low, high) in zip(planes, layout):
        picked += [value[:low], value[count - high :]]
    return jnp.concatenate(picked, axis=0)


def rest(planes, layout):
    inner = [value[low : count - high] for value, (_, count, low, high) in zip(planes, layout)]
    inner = jnp.concatenate(inner, axis=0)
    missing = 29 - inner.shape[0]
    if missing:
        inner = jnp.concatenate([inner, jnp.zeros((missing, 8, 128), jnp.float32)], axis=0)
    return inner[AHEAD - 37 :]


def local_kernel(eps_ref, e, h, g, kf, m, next_ref, pair_ref, late0, late1, t1s, s1s, s0s, cs):
    even_x = lax.axis_index("c") == 0
    even_z = lax.axis_index("x") % 2 == 0
    x_flag = low_flag(XY)
    values = coefs(eps_ref)

    def below(row, z):
        return jnp.where(even_x, next_ref[row, plane(z), :], pair_ref[row, plane(z), :])[None]

    def above(row, z):
        return jnp.where(even_x, pair_ref[row, plane(z), :], next_ref[row, plane(z), :])[None]

    def extended(ref, base, comp, z):
        row = base + comp * 2
        return jnp.concatenate(
            [below(row, z), below(row + 1, z), ref[comp, :, plane(z), :], above(row, z), above(row + 1, z)],
            axis=0,
        )

    coef = []
    for z in range(2):
        own = table(m[:, plane(z), :], values)
        coef.append(jnp.concatenate([below(24, z), below(25, z), own, above(24, z), above(25, z)], axis=0))
        cs[z] = coef[z][1:11]

    for chain in range(2):
        alpha, beta = ALPHA[chain], BETA[chain]
        if chain == 0:
            s = [[extended(e, 0, comp, z) for z in range(2)] for comp in range(3)]
            t = [[extended(h, 6, comp, z)[:11] for z in range(2)] for comp in range(3)]
        else:
            s = [[extended(g, 12, comp, z) * coef[z] for z in range(2)] for comp in range(3)]
            t = [[extended(kf, 18, comp, z)[:11] for z in range(2)] for comp in range(3)]
        sx, sy, sz = s
        t1 = [[None, None] for _ in range(3)]
        for z in range(2):
            dz_y = (sy[1] - sy[0])[:11] if z == 0 else -sy[1][:11]
            dz_x = (sx[1] - sx[0])[:11] if z == 0 else -sx[1][:11]
            t1[0][z] = t[0][z] + alpha * (ahead_y(sz[z][:11]) - dz_y)
            t1[1][z] = t[1][z] + alpha * (dz_x - (sz[z][1:] - sz[z][:11]))
            t1[2][z] = t[2][z] + alpha * ((sy[z][1:] - sy[z][:11]) - ahead_y(sx[z][:11]))
            for comp in range(3):
                t1[comp][z] = keep_low(t1[comp][z], 2, x_flag)
                t1s[chain, comp, z] = t1[comp][z]
        s1 = [[None, None] for _ in range(3)]
        for z in range(2):
            tx, ty, tz = t1[0][z], t1[1][z], t1[2][z]
            b = beta * coef[z][1:11]
            dz_y = ty[1:] if z == 0 else (ty - t1[1][0])[1:]
            dz_x = tx[1:] if z == 0 else (tx - t1[0][0])[1:]
            s1[0][z] = sx[z][1:11] + b * (behind_y(tz[1:]) - dz_y)
            s1[1][z] = sy[z][1:11] + b * (dz_x - (tz[1:] - tz[:10]))
            s1[2][z] = sz[z][1:11] + b * ((ty[1:] - ty[:10]) - behind_y(tx[1:]))
            for comp in range(3):
                s1s[chain, comp, z] = s1[comp][z]
        s0s[chain, 0] = sx[0][1:11]
        s0s[chain, 1] = sy[0][1:11]
        ax, ay = t1[0][1][1:], t1[1][1][1:]
        px = ax[1:9] + alpha * (ahead_y(s1[2][1][1:9]) + s1[1][1][1:9])
        py = ay[1:9] - alpha * (s1[0][1][1:9] + (s1[2][1][2:10] - s1[2][1][1:9]))
        up = (ax, ay, px, py)
        down = (sx[0][:11], sy[0][1:11], s1[0][0][:9], s1[1][0][1:9])
        late_up = edges(up, UP)
        late_down = jnp.concatenate([edges(down, DOWN), jnp.zeros((1, 8, 128), jnp.float32)], axis=0)
        late0[pl.ds(10 * chain, 10)] = jnp.where(even_z, late_up, late_down)
        late1[pl.ds(10 * chain, 10)] = jnp.where(even_z, late_down, late_up)
    late0[pl.ds(LATE, EARLY - AHEAD)] = jnp.where(even_z, rest(up, UP), rest(down, DOWN))
    late0[20] = jnp.where(even_z, coef[1][10], coef[0][1])
    late1[20] = jnp.where(even_z, coef[0][1], coef[1][10])


def take_kernel(*refs):
    del refs


def final_kernel(eps_ref, e, g, m, owner, early1, early0, late1, late0, t1s, s1s, s0s, cs, adj_e, adj_h, sums):
    even_z = lax.axis_index("x") % 2 == 0
    x_flag, z_flag = low_flag(XY), low_flag(GZ)
    values = coefs(eps_ref)
    inverse = [2.0 * eps_ref[kind] for kind in range(4)]

    def early_even(start, count):
        ahead = max(0, min(count, AHEAD - start))
        parts = [early0[pl.ds(start, ahead)]] if ahead else []
        if ahead < count:
            parts.append(late0[pl.ds(LATE + start + ahead - AHEAD, count - ahead)])
        return jnp.concatenate(parts, axis=0)

    def early_up(start, count):
        return jnp.where(even_z, early_even(start, count), early1[pl.ds(start, count)])

    def early_low(start, count):
        return jnp.where(even_z, early1[pl.ds(start, count)], early_even(start, count))

    def late_up(start, count):
        return jnp.where(even_z, late0[pl.ds(start, count)], late1[pl.ds(start, count)])

    def late_low(start, count):
        return jnp.where(even_z, late1[pl.ds(start, count)], late0[pl.ds(start, count)])

    def joined(early_lines, late_lines, layout, chain, at):
        first, edge = 37 * chain, 10 * chain
        for _, count, low, high in layout[:at]:
            first, edge = first + count - low - high, edge + low + high
        _, count, low, high = layout[at]
        middle = early_lines(first, count - low - high)
        return jnp.concatenate([late_lines(edge, low), middle, late_lines(edge + low, high)], axis=0)

    c_up = jnp.concatenate([late_up(20, 1), early_up(29, 8)], axis=0)
    c_low = jnp.concatenate([early_low(29, 8), late_low(20, 1)], axis=0)
    own = slice(1, 9)
    kept = []
    for chain in range(2):
        alpha, beta = ALPHA[chain], BETA[chain]
        sx2, sy2, qx, qy = (joined(early_up, late_up, DOWN, chain, at) for at in range(4))
        ax, ay, px, py = (joined(early_low, late_low, UP, chain, at) for at in range(4))
        sx0, sy0 = s0s[chain, 0], s0s[chain, 1]
        tx = [t1s[chain, 0, 0][1:], t1s[chain, 0, 1][1:] - alpha * sy2]
        ty = [t1s[chain, 1, 0][1:], t1s[chain, 1, 1][1:] + alpha * sx2[1:]]
        tz = [t1s[chain, 2, 0][1:], t1s[chain, 2, 1][1:]]
        tx_low = (ax - alpha * sy0) * z_flag
        ty_low = (ay + alpha * sx0) * z_flag
        b0, b1 = beta * cs[0], beta * cs[1]
        div2 = (sx2[1:] - sx2[:10]) + behind_y(sy2)
        sx = [s1s[chain, 0, 0] + b0 * ty_low, s1s[chain, 0, 1] - alpha * b1 * sx2[1:]]
        sy = [s1s[chain, 1, 0] - b0 * tx_low, s1s[chain, 1, 1] - alpha * b1 * sy2]
        sz = [s1s[chain, 2, 0], s1s[chain, 2, 1] + alpha * b1 * div2]
        b_up, b_low = beta * c_up, beta * c_low
        sx.append(qx + b_up * ty[1][:9])
        sy_top = qy - b_up[1:] * tx[1][own]
        t2x, t2y, t2z = [], [], []
        for z in range(2):
            dz_y = (sy[1] - sy[0])[own] if z == 0 else sy_top - sy[1][own]
            dz_x = sx[z + 1][:9] - sx[z][:9]
            t2x.append(tx[z][own] + alpha * (ahead_y(sz[z][own]) - dz_y))
            y_new = ty[z][:9] + alpha * (dz_x - (sz[z][1:] - sz[z][:9]))
            z_new = tz[z][:9] + alpha * ((sy[z][1:] - sy[z][:9]) - ahead_y(sx[z][:9]))
            t2y.append(keep_low(y_new, 1, x_flag))
            t2z.append(keep_low(z_new, 1, x_flag))
        div0 = b_low * ((sx0[1:] - sx0[:9]) + behind_y(sy0[1:]))
        x_low = px - alpha * (sy0[own] + sy[0][own]) + alpha * alpha * (ahead_y(div0[:8]) - b_low[:8] * sy0[own])
        y_low = py + alpha * (sx0[own] + sx[0][own]) + alpha * alpha * (b_low[:8] * sx0[own] - (div0[1:] - div0[:8]))
        x_low, y_low = x_low * z_flag, y_low * z_flag
        curl = []
        for z in range(2):
            dz_y = t2y[z][1:] - (y_low if z == 0 else t2y[0][1:])
            dz_x = t2x[z] - (x_low if z == 0 else t2x[0])
            curl.append((
                behind_y(t2z[z][1:]) - dz_y,
                dz_x - (t2z[z][1:] - t2z[z][:8]),
                (t2y[z][1:] - t2y[z][:8]) - behind_y(t2x[z]),
            ))
        kept.append(([[s[z][own] for s in (sx, sy, sz)] for z in range(2)], curl))
        if chain == 1:
            for z in range(2):
                scale = table(m[:, plane(z), :], inverse)
                for comp, t2 in enumerate((t2x[z], t2y[z][1:], t2z[z][1:])):
                    adj_e[comp, :, plane(z), :] = kept[1][0][z][comp] * scale - COURANT * curl[z][comp]
                    adj_h[comp, :, plane(z), :] = t2

    totals = [jnp.zeros((8, 128), jnp.float32) for _ in range(NI)]
    for z in range(2):
        coef = table(m[:, plane(z), :], values)
        weight = jnp.zeros((8, 8, 128), jnp.float32)
        for comp in range(3):
            step = kept[0][0][z][comp] - e[comp, :, plane(z), :]
            weight = weight + kept[1][0][z][comp] * step
            weight = weight + coef * g[comp, :, plane(z), :] * (coef * kept[0][1][z][comp])
        who = owner[:, plane(z), :]
        for j in range(NI):
            totals[j] = totals[j] + jnp.sum(jnp.where(who == j, weight, 0.0), axis=0)
    lane = lax.broadcasted_iota(jnp.int32, (1, 128), 1)
    row = jnp.zeros((1, 128), jnp.float32)
    for j in range(NI):
        row = row + jnp.where(lane == j, jnp.sum(totals[j]), 0.0)
    sums[...] = jnp.broadcast_to(row, sums.shape)


VMEM = pl.BlockSpec(memory_space=pltpu.VMEM)
SMEM = pl.BlockSpec(memory_space=pltpu.SMEM)
ANY = pl.BlockSpec(memory_space=pl.ANY)
HBM = pl.BlockSpec(memory_space=pltpu.HBM)
TAKE = 2 * 10**10
LARGE = 62 * 1024 * 1024
PARAMS = pltpu.CompilerParams(vmem_limit_bytes=48 * 1024 * 1024)


def f32(*shape):
    return jax.ShapeDtypeStruct(shape, jnp.float32)


def rows(u):
    lead = u.shape[:-2]
    n = len(lead)
    return u.reshape(*lead, 2, 8, 128).transpose(*range(n), n + 1, n, n + 2).reshape(*lead, 16, 128)


def unrows(u):
    lead = u.shape[:-2]
    n = len(lead)
    return u.reshape(*lead, 8, 2, 128).transpose(*range(n), n + 1, n, n + 2).reshape(*lead, 2, 1024)


def swap_pairs(value, axes, odd):
    size = lax.axis_size(axes)
    pairs = []
    for low in range(odd, size - 1, 2):
        pairs += [(low, low + 1), (low + 1, low)]
    return lax.ppermute(value, axes, pairs)


def spread_sum(value, axes):
    size = lax.axis_size(axes)
    sent = jnp.broadcast_to(value[None], (size, value.shape[0]))
    return jnp.sum(lax.all_to_all(sent, axes, 0, 0), axis=0)


def body(e_check, h_check, adj_e, adj_h, material, owner, permittivity):
    e, h, g, k, m, own = (rows(u) for u in (e_check, h_check, adj_e, adj_h, material, owner))
    pair, following, early0, early1 = pl.pallas_call(
        pack_kernel,
        out_shape=(f32(HALO, 16, 128), f32(HALO, 16, 128), f32(AHEAD, 8, 128), f32(EARLY, 8, 128)),
        in_specs=[HBM] * 6,
        out_specs=[VMEM] * 4,
        scratch_shapes=[
            pltpu.SMEM((4,), jnp.float32),
            pltpu.VMEM((4, 3, 8, 16, 128), jnp.float32),
            pltpu.VMEM((8, 16, 128), jnp.int32),
            pltpu.SemaphoreType.DMA((6,)),
        ],
        compiler_params=pltpu.CompilerParams(vmem_limit_bytes=LARGE),
        name="pack",
    )(permittivity, e, h, g, k, m)
    early1 = swap_pairs(early1, GZ, 1)
    early0 = swap_pairs(early0, "x", 0)
    pair = swap_pairs(pair, "c", 0)
    following = swap_pairs(following, XY, 1)
    late0, late1, t1s, s1s, s0s, cs = pl.pallas_call(
        local_kernel,
        out_shape=(
            f32(LATE + EARLY - AHEAD, 8, 128),
            f32(LATE, 8, 128),
            f32(2, 3, 2, 11, 8, 128),
            f32(2, 3, 2, 10, 8, 128),
            f32(2, 2, 10, 8, 128),
            f32(2, 10, 8, 128),
        ),
        in_specs=[SMEM] + [VMEM] * 7,
        out_specs=[VMEM] * 6,
        compiler_params=PARAMS,
        cost_estimate=pl.CostEstimate(flops=1, bytes_accessed=1, transcendentals=0),
        name="local_step",
    )(permittivity, e, h, g, k, m, following, pair)
    late0 = swap_pairs(late0, "x", 0)
    late1 = swap_pairs(late1, GZ, 1)
    early1, early0 = pl.pallas_call(
        take_kernel,
        out_shape=(f32(EARLY, 8, 128), f32(AHEAD, 8, 128)),
        in_specs=[ANY] * 2,
        out_specs=[ANY] * 2,
        input_output_aliases={0: 0, 1: 1},
        compiler_params=PARAMS,
        cost_estimate=pl.CostEstimate(flops=TAKE, bytes_accessed=10**9, transcendentals=0),
        name="take_early",
    )(early1, early0)
    out_e, out_h, sums = pl.pallas_call(
        final_kernel,
        out_shape=(f32(3, 8, 16, 128), f32(3, 8, 16, 128), f32(1, 128)),
        in_specs=[SMEM] + [VMEM] * 12,
        out_specs=[VMEM] * 3,
        compiler_params=PARAMS,
        name="final_step",
    )(permittivity, e, g, m, own, early1, early0, late1, late0, t1s, s1s, s0s, cs)
    total = spread_sum(sums[0], ("zl", "zh", "c"))
    total = spread_sum(total, ("y", "x"))
    cells = 8 * lax.axis_size(XY) * 2 * lax.axis_size(GZ) * 1024
    gradient = total[:NI] / jnp.sqrt(jnp.float32(cells / NI))
    return unrows(out_e), unrows(out_h), gradient


def on_split(split):
    return jax.shard_map(
        body,
        mesh=split,
        in_specs=(P(None, XY, GZ, None),) * 4 + (P(XY, GZ, None),) * 2 + (P(),),
        out_specs=(P(None, XY, GZ, None), P(None, XY, GZ, None), P()),
        check_vma=False,
    )


def solution(mesh):
    return on_split(Mesh(mesh.devices.reshape(4, 8, 2, 2, 4), AXES))
```

```python
import functools

import jax
import jax.numpy as jnp
from jax import lax
from jax.experimental import pallas as pl
from jax.experimental.pallas import tpu as pltpu
from jax.sharding import Mesh
from jax.sharding import PartitionSpec as P

NI = 8
AXES = ("zl", "y", "c", "zh", "x")
XY = ("zl", "y", "c")
GZ = ("zh", "x")
COURANT = 0.5
ALPHA = (-COURANT, 1.0)
BETA = (1.0, -COURANT)

UP = (("ax", 10, 1, 1), ("ay", 10, 1, 2), ("px", 8, 1, 1), ("py", 8, 1, 2))
DOWN = (("sx", 11, 2, 1), ("sy", 10, 1, 1), ("qx", 9, 1, 1), ("qy", 8, 1, 1))
EARLY = 2 * 29 + 8
LATE = 2 * 10 + 1
AHEAD = 40
HALO = 13


def shift_later(u):
    lane = lax.broadcasted_iota(jnp.int32, u.shape, u.ndim - 1)
    row = lax.broadcasted_iota(jnp.int32, u.shape, u.ndim - 2)
    turned = pltpu.roll(u, 127, u.ndim - 1)
    carried = pltpu.roll(turned, 7, u.ndim - 2)
    return jnp.where(lane < 127, turned, jnp.where(row < 7, carried, 0.0))


def shift_earlier(u):
    lane = lax.broadcasted_iota(jnp.int32, u.shape, u.ndim - 1)
    row = lax.broadcasted_iota(jnp.int32, u.shape, u.ndim - 2)
    turned = pltpu.roll(u, 1, u.ndim - 1)
    carried = pltpu.roll(turned, 1, u.ndim - 2)
    return jnp.where(lane > 0, turned, jnp.where(row > 0, carried, 0.0))


def ahead_y(u):
    return shift_later(u) - u


def behind_y(u):
    return u - shift_earlier(u)


def table(material, values):
    out = jnp.zeros(material.shape, jnp.float32)
    for kind in range(4):
        out = out + jnp.where(material == kind, values[kind], 0.0)
    return out


def coefs(eps_ref):
    return [COURANT / eps_ref[kind] for kind in range(4)]


def plane(z):
    return pl.ds(z, 8, stride=2)


def keep_low(u, count, flag):
    return jnp.concatenate([u[:count] * flag, u[count:]], axis=0)


def low_flag(axes):
    first = functools.reduce(jnp.logical_and, [lax.axis_index(a) == 0 for a in axes])
    return jnp.where(first, 0.0, 1.0).astype(jnp.float32)


def pack_kernel(eps_ref, e, h, g, k, m, pair_ref, next_ref, early0, early1, eps, fields, kinds, edge, lines0, lines1, sems, outs):
    kinds_in = pltpu.make_async_copy(m, kinds, sems.at[4])
    eps_in = pltpu.make_async_copy(eps_ref, eps, sems.at[5])
    fields_in = [pltpu.make_async_copy(ref, fields.at[i], sems.at[i]) for i, ref in enumerate((e, h, g, k))]
    for copy in (kinds_in, eps_in, *fields_in):
        copy.start()
    even = lax.axis_index("c") == 0
    even_z = lax.axis_index("x") % 2 == 0
    sides = ((jnp.where(even, 6, 0), pair_ref), (jnp.where(even, 0, 6), next_ref))
    sent = []

    def send(source, target, at):
        sent.append(pltpu.make_async_copy(source, target, outs.at[at]))
        sent[-1].start()

    kinds_in.wait()
    eps_in.wait()
    values = coefs(eps)
    for side, (start, out) in enumerate(sides):
        edge[side] = table(kinds[pl.ds(start, 2)], values)
        send(edge.at[side], out.at[12], side * 5 + 4)
    for field, copy in enumerate(fields_in):
        copy.wait()
        for side, (start, out) in enumerate(sides):
            send(fields.at[field, :, pl.ds(start, 2)], out.at[3 * field : 3 * field + 3], side * 5 + field)

    coef = [table(kinds[:, plane(z), :], values) for z in range(2)]
    ups, downs = [], []
    for chain in range(2):
        alpha, beta = ALPHA[chain], BETA[chain]

        def load(field, comp, z):
            return fields[field, comp, :, plane(z), :]

        s = [[load(2 * chain, comp, z) for z in range(2)] for comp in range(3)]
        if chain == 1:
            s = [[s[comp][z] * coef[z] for z in range(2)] for comp in range(3)]
        sx, sy, sz = s
        tx, ty, tz = [], [], []
        for z in range(2):
            dz_y = sy[1] - sy[0] if z == 0 else -sy[1]
            dz_x = sx[1] - sx[0] if z == 0 else -sx[1]
            tx.append(load(2 * chain + 1, 0, z) + alpha * (ahead_y(sz[z]) - dz_y))
            ty.append(load(2 * chain + 1, 1, z)[:7] + alpha * (dz_x[:7] - (sz[z][1:] - sz[z][:7])))
            tz.append(load(2 * chain + 1, 2, z)[:7] + alpha * ((sy[z][1:] - sy[z][:7]) - ahead_y(sx[z][:7])))
        b0, b1 = beta * coef[0], beta * coef[1]
        qx = sx[0][:7] + b0[:7] * (behind_y(tz[0]) - ty[0])
        qy = sy[0][1:7] + b0[1:7] * (tx[0][1:7] - (tz[0][1:] - tz[0][:6]))
        s1x = sx[1][:7] + b1[:7] * (behind_y(tz[1]) - (ty[1] - ty[0]))
        s1y = sy[1][1:7] + b1[1:7] * ((tx[1] - tx[0])[1:7] - (tz[1][1:] - tz[1][:6]))
        s1z = sz[1][1:7] + b1[1:7] * ((ty[1][1:] - ty[1][:6]) - behind_y(tx[1][1:7]))
        px = tx[1][1:7] + alpha * (ahead_y(s1z) + s1y)
        py = ty[1][1:6] - alpha * (s1x[1:6] + (s1z[1:] - s1z[:5]))
        ups += [tx[1], ty[1], px, py, jnp.zeros((3, 8, 128), jnp.float32)]
        downs += [sx[0], sy[0], qx, qy]
        if chain == 0:
            ups.append(coef[1])
            downs.append(coef[0])
    up, down = jnp.concatenate(ups, axis=0), jnp.concatenate(downs, axis=0)
    lines1[...] = jnp.where(even_z, down, up)
    send(lines1, early1, 10)
    lines0[...] = jnp.where(even_z, up, down)[:AHEAD]
    send(lines0, early0, 11)
    for copy in sent:
        copy.wait()


def edges(planes, layout):
    picked = []
    for value, (_, count, low, high) in zip(planes, layout):
        picked += [value[:low], value[count - high :]]
    return jnp.concatenate(picked, axis=0)


def rest(planes, layout):
    inner = [value[low : count - high] for value, (_, count, low, high) in zip(planes, layout)]
    inner = jnp.concatenate(inner, axis=0)
    missing = 29 - inner.shape[0]
    if missing:
        inner = jnp.concatenate([inner, jnp.zeros((missing, 8, 128), jnp.float32)], axis=0)
    return inner[AHEAD - 37 :]


def local_kernel(eps_ref, e, h, g, kf, m, next_ref, pair_ref, late0, late1, t1s, s1s, s0s, cs):
    even_x = lax.axis_index("c") == 0
    even_z = lax.axis_index("x") % 2 == 0
    x_flag = low_flag(XY)
    values = coefs(eps_ref)

    def below(row, z):
        return jnp.where(even_x, next_ref[row // 2, row % 2, plane(z), :], pair_ref[row // 2, row % 2, plane(z), :])[None]

    def above(row, z):
        return jnp.where(even_x, pair_ref[row // 2, row % 2, plane(z), :], next_ref[row // 2, row % 2, plane(z), :])[None]

    def extended(ref, base, comp, z):
        row = base + comp * 2
        return jnp.concatenate(
            [below(row, z), below(row + 1, z), ref[comp, :, plane(z), :], above(row, z), above(row + 1, z)],
            axis=0,
        )

    coef = []
    for z in range(2):
        own = table(m[:, plane(z), :], values)
        coef.append(jnp.concatenate([below(24, z), below(25, z), own, above(24, z), above(25, z)], axis=0))
        cs[z] = coef[z][1:11]

    for chain in range(2):
        alpha, beta = ALPHA[chain], BETA[chain]
        if chain == 0:
            s = [[extended(e, 0, comp, z) for z in range(2)] for comp in range(3)]
            t = [[extended(h, 6, comp, z)[:11] for z in range(2)] for comp in range(3)]
        else:
            s = [[extended(g, 12, comp, z) * coef[z] for z in range(2)] for comp in range(3)]
            t = [[extended(kf, 18, comp, z)[:11] for z in range(2)] for comp in range(3)]
        sx, sy, sz = s
        t1 = [[None, None] for _ in range(3)]
        for z in range(2):
            dz_y = (sy[1] - sy[0])[:11] if z == 0 else -sy[1][:11]
            dz_x = (sx[1] - sx[0])[:11] if z == 0 else -sx[1][:11]
            t1[0][z] = t[0][z] + alpha * (ahead_y(sz[z][:11]) - dz_y)
            t1[1][z] = t[1][z] + alpha * (dz_x - (sz[z][1:] - sz[z][:11]))
            t1[2][z] = t[2][z] + alpha * ((sy[z][1:] - sy[z][:11]) - ahead_y(sx[z][:11]))
            for comp in range(3):
                t1[comp][z] = keep_low(t1[comp][z], 2, x_flag)
                t1s[chain, comp, z] = t1[comp][z]
        s1 = [[None, None] for _ in range(3)]
        for z in range(2):
            tx, ty, tz = t1[0][z], t1[1][z], t1[2][z]
            b = beta * coef[z][1:11]
            dz_y = ty[1:] if z == 0 else (ty - t1[1][0])[1:]
            dz_x = tx[1:] if z == 0 else (tx - t1[0][0])[1:]
            s1[0][z] = sx[z][1:11] + b * (behind_y(tz[1:]) - dz_y)
            s1[1][z] = sy[z][1:11] + b * (dz_x - (tz[1:] - tz[:10]))
            s1[2][z] = sz[z][1:11] + b * ((ty[1:] - ty[:10]) - behind_y(tx[1:]))
            for comp in range(3):
                s1s[chain, comp, z] = s1[comp][z]
        s0s[chain, 0] = sx[0][1:11]
        s0s[chain, 1] = sy[0][1:11]
        ax, ay = t1[0][1][1:], t1[1][1][1:]
        px = ax[1:9] + alpha * (ahead_y(s1[2][1][1:9]) + s1[1][1][1:9])
        py = ay[1:9] - alpha * (s1[0][1][1:9] + (s1[2][1][2:10] - s1[2][1][1:9]))
        up = (ax, ay, px, py)
        down = (sx[0][:11], sy[0][1:11], s1[0][0][:9], s1[1][0][1:9])
        late_up = edges(up, UP)
        late_down = jnp.concatenate([edges(down, DOWN), jnp.zeros((1, 8, 128), jnp.float32)], axis=0)
        late0[pl.ds(10 * chain, 10)] = jnp.where(even_z, late_up, late_down)
        late1[pl.ds(10 * chain, 10)] = jnp.where(even_z, late_down, late_up)
    late0[pl.ds(LATE, EARLY - AHEAD)] = jnp.where(even_z, rest(up, UP), rest(down, DOWN))
    late0[20] = jnp.where(even_z, coef[1][10], coef[0][1])
    late1[20] = jnp.where(even_z, coef[0][1], coef[1][10])


def take_kernel(*refs):
    del refs


def final_kernel(eps_ref, e, g, m, owner, early1, early0, late1, late0, t1s, s1s, s0s, cs, adj_e, adj_h, sums, new_e, new_h, outs):
    even_z = lax.axis_index("x") % 2 == 0
    x_flag, z_flag = low_flag(XY), low_flag(GZ)
    values = coefs(eps_ref)
    inverse = [2.0 * eps_ref[kind] for kind in range(4)]

    def early_even(start, count):
        ahead = max(0, min(count, AHEAD - start))
        parts = [early0[pl.ds(start, ahead)]] if ahead else []
        if ahead < count:
            parts.append(late0[pl.ds(LATE + start + ahead - AHEAD, count - ahead)])
        return jnp.concatenate(parts, axis=0)

    def early_up(start, count):
        return jnp.where(even_z, early_even(start, count), early1[pl.ds(start, count)])

    def early_low(start, count):
        return jnp.where(even_z, early1[pl.ds(start, count)], early_even(start, count))

    def late_up(start, count):
        return jnp.where(even_z, late0[pl.ds(start, count)], late1[pl.ds(start, count)])

    def late_low(start, count):
        return jnp.where(even_z, late1[pl.ds(start, count)], late0[pl.ds(start, count)])

    def joined(early_lines, late_lines, layout, chain, at):
        first, edge = 37 * chain, 10 * chain
        for _, count, low, high in layout[:at]:
            first, edge = first + count - low - high, edge + low + high
        _, count, low, high = layout[at]
        middle = early_lines(first, count - low - high)
        return jnp.concatenate([late_lines(edge, low), middle, late_lines(edge + low, high)], axis=0)

    c_up = jnp.concatenate([late_up(20, 1), early_up(29, 8)], axis=0)
    c_low = jnp.concatenate([early_low(29, 8), late_low(20, 1)], axis=0)
    own = slice(1, 9)
    kept = [None, None]
    writes = [pltpu.make_async_copy(new_e, adj_e, outs.at[0]), pltpu.make_async_copy(new_h, adj_h, outs.at[1])]
    for chain in (1, 0):
        alpha, beta = ALPHA[chain], BETA[chain]
        sx2, sy2, qx, qy = (joined(early_up, late_up, DOWN, chain, at) for at in range(4))
        ax, ay, px, py = (joined(early_low, late_low, UP, chain, at) for at in range(4))
        sx0, sy0 = s0s[chain, 0], s0s[chain, 1]
        tx = [t1s[chain, 0, 0][1:], t1s[chain, 0, 1][1:] - alpha * sy2]
        ty = [t1s[chain, 1, 0][1:], t1s[chain, 1, 1][1:] + alpha * sx2[1:]]
        tz = [t1s[chain, 2, 0][1:], t1s[chain, 2, 1][1:]]
        tx_low = (ax - alpha * sy0) * z_flag
        ty_low = (ay + alpha * sx0) * z_flag
        b0, b1 = beta * cs[0], beta * cs[1]
        div2 = (sx2[1:] - sx2[:10]) + behind_y(sy2)
        sx = [s1s[chain, 0, 0] + b0 * ty_low, s1s[chain, 0, 1] - alpha * b1 * sx2[1:]]
        sy = [s1s[chain, 1, 0] - b0 * tx_low, s1s[chain, 1, 1] - alpha * b1 * sy2]
        sz = [s1s[chain, 2, 0], s1s[chain, 2, 1] + alpha * b1 * div2]
        b_up, b_low = beta * c_up, beta * c_low
        sx.append(qx + b_up * ty[1][:9])
        sy_top = qy - b_up[1:] * tx[1][own]
        t2x, t2y, t2z = [], [], []
        for z in range(2):
            dz_y = (sy[1] - sy[0])[own] if z == 0 else sy_top - sy[1][own]
            dz_x = sx[z + 1][:9] - sx[z][:9]
            t2x.append(tx[z][own] + alpha * (ahead_y(sz[z][own]) - dz_y))
            y_new = ty[z][:9] + alpha * (dz_x - (sz[z][1:] - sz[z][:9]))
            z_new = tz[z][:9] + alpha * ((sy[z][1:] - sy[z][:9]) - ahead_y(sx[z][:9]))
            t2y.append(keep_low(y_new, 1, x_flag))
            t2z.append(keep_low(z_new, 1, x_flag))
        div0 = b_low * ((sx0[1:] - sx0[:9]) + behind_y(sy0[1:]))
        x_low = px - alpha * (sy0[own] + sy[0][own]) + alpha * alpha * (ahead_y(div0[:8]) - b_low[:8] * sy0[own])
        y_low = py + alpha * (sx0[own] + sx[0][own]) + alpha * alpha * (b_low[:8] * sx0[own] - (div0[1:] - div0[:8]))
        x_low, y_low = x_low * z_flag, y_low * z_flag
        curl = []
        for z in range(2):
            dz_y = t2y[z][1:] - (y_low if z == 0 else t2y[0][1:])
            dz_x = t2x[z] - (x_low if z == 0 else t2x[0])
            curl.append((
                behind_y(t2z[z][1:]) - dz_y,
                dz_x - (t2z[z][1:] - t2z[z][:8]),
                (t2y[z][1:] - t2y[z][:8]) - behind_y(t2x[z]),
            ))
        kept[chain] = ([[s[z][own] for s in (sx, sy, sz)] for z in range(2)], curl)
        if chain == 1:
            for z in range(2):
                scale = table(m[:, plane(z), :], inverse)
                for comp, t2 in enumerate((t2x[z], t2y[z][1:], t2z[z][1:])):
                    new_e[comp, :, plane(z), :] = kept[1][0][z][comp] * scale - COURANT * curl[z][comp]
                    new_h[comp, :, plane(z), :] = t2
            for copy in writes:
                copy.start()

    totals = [jnp.zeros((8, 128), jnp.float32) for _ in range(NI)]
    for z in range(2):
        coef = table(m[:, plane(z), :], values)
        weight = jnp.zeros((8, 8, 128), jnp.float32)
        for comp in range(3):
            step = kept[0][0][z][comp] - e[comp, :, plane(z), :]
            weight = weight + kept[1][0][z][comp] * step
            weight = weight + coef * g[comp, :, plane(z), :] * (coef * kept[0][1][z][comp])
        who = owner[:, plane(z), :]
        for j in range(NI):
            totals[j] = totals[j] + jnp.sum(jnp.where(who == j, weight, 0.0), axis=0)
    lane = lax.broadcasted_iota(jnp.int32, (1, 128), 1)
    row = jnp.zeros((1, 128), jnp.float32)
    for j in range(NI):
        row = row + jnp.where(lane == j, jnp.sum(totals[j]), 0.0)
    sums[...] = jnp.broadcast_to(row, sums.shape)
    for copy in writes:
        copy.wait()


VMEM = pl.BlockSpec(memory_space=pltpu.VMEM)
SMEM = pl.BlockSpec(memory_space=pltpu.SMEM)
ANY = pl.BlockSpec(memory_space=pl.ANY)
HBM = pl.BlockSpec(memory_space=pltpu.HBM)
TAKE = 2 * 10**10
LARGE = 62 * 1024 * 1024
PARAMS = pltpu.CompilerParams(vmem_limit_bytes=48 * 1024 * 1024)


def f32(*shape):
    return jax.ShapeDtypeStruct(shape, jnp.float32)


def rows(u):
    lead = u.shape[:-2]
    n = len(lead)
    return u.reshape(*lead, 2, 8, 128).transpose(*range(n), n + 1, n, n + 2).reshape(*lead, 16, 128)


def unrows(u):
    lead = u.shape[:-2]
    n = len(lead)
    return u.reshape(*lead, 8, 2, 128).transpose(*range(n), n + 1, n, n + 2).reshape(*lead, 2, 1024)


def swap_pairs(value, axes, odd):
    size = lax.axis_size(axes)
    pairs = []
    for low in range(odd, size - 1, 2):
        pairs += [(low, low + 1), (low + 1, low)]
    return lax.ppermute(value, axes, pairs)


def spread_sum(value, axes):
    size = lax.axis_size(axes)
    sent = jnp.broadcast_to(value[None], (size, value.shape[0]))
    return jnp.sum(lax.all_to_all(sent, axes, 0, 0), axis=0)


def body(e_check, h_check, adj_e, adj_h, material, owner, permittivity):
    e, h, g, k, m, own = (rows(u) for u in (e_check, h_check, adj_e, adj_h, material, owner))
    pair, following, early0, early1 = pl.pallas_call(
        pack_kernel,
        out_shape=(f32(HALO, 2, 16, 128), f32(HALO, 2, 16, 128), f32(AHEAD, 8, 128), f32(EARLY, 8, 128)),
        in_specs=[HBM] * 6,
        out_specs=[HBM] * 4,
        scratch_shapes=[
            pltpu.SMEM((4,), jnp.float32),
            pltpu.VMEM((4, 3, 8, 16, 128), jnp.float32),
            pltpu.VMEM((8, 16, 128), jnp.int32),
            pltpu.VMEM((2, 2, 16, 128), jnp.float32),
            pltpu.VMEM((AHEAD, 8, 128), jnp.float32),
            pltpu.VMEM((EARLY, 8, 128), jnp.float32),
            pltpu.SemaphoreType.DMA((6,)),
            pltpu.SemaphoreType.DMA((12,)),
        ],
        compiler_params=pltpu.CompilerParams(vmem_limit_bytes=LARGE),
        name="pack",
    )(permittivity, e, h, g, k, m)
    early1 = swap_pairs(early1, GZ, 1)
    early0 = swap_pairs(early0, "x", 0)
    pair = swap_pairs(pair, "c", 0)
    following = swap_pairs(following, XY, 1)
    late0, late1, t1s, s1s, s0s, cs = pl.pallas_call(
        local_kernel,
        out_shape=(
            f32(LATE + EARLY - AHEAD, 8, 128),
            f32(LATE, 8, 128),
            f32(2, 3, 2, 11, 8, 128),
            f32(2, 3, 2, 10, 8, 128),
            f32(2, 2, 10, 8, 128),
            f32(2, 10, 8, 128),
        ),
        in_specs=[SMEM] + [VMEM] * 7,
        out_specs=[VMEM] * 6,
        compiler_params=PARAMS,
        cost_estimate=pl.CostEstimate(flops=1, bytes_accessed=1, transcendentals=0),
        name="local_step",
    )(permittivity, e, h, g, k, m, following, pair)
    late0 = swap_pairs(late0, "x", 0)
    late1 = swap_pairs(late1, GZ, 1)
    early1, early0 = pl.pallas_call(
        take_kernel,
        out_shape=(f32(EARLY, 8, 128), f32(AHEAD, 8, 128)),
        in_specs=[ANY] * 2,
        out_specs=[ANY] * 2,
        input_output_aliases={0: 0, 1: 1},
        compiler_params=PARAMS,
        cost_estimate=pl.CostEstimate(flops=TAKE, bytes_accessed=10**9, transcendentals=0),
        name="take_early",
    )(early1, early0)
    out_e, out_h, sums = pl.pallas_call(
        final_kernel,
        out_shape=(f32(3, 8, 16, 128), f32(3, 8, 16, 128), f32(1, 128)),
        in_specs=[SMEM] + [VMEM] * 12,
        out_specs=[HBM, HBM, VMEM],
        scratch_shapes=[
            pltpu.VMEM((3, 8, 16, 128), jnp.float32),
            pltpu.VMEM((3, 8, 16, 128), jnp.float32),
            pltpu.SemaphoreType.DMA((2,)),
        ],
        compiler_params=PARAMS,
        name="final_step",
    )(permittivity, e, g, m, own, early1, early0, late1, late0, t1s, s1s, s0s, cs)
    total = spread_sum(sums[0], ("zl", "zh", "c"))
    total = spread_sum(total, ("y", "x"))
    cells = 8 * lax.axis_size(XY) * 2 * lax.axis_size(GZ) * 1024
    gradient = total[:NI] / jnp.sqrt(jnp.float32(cells / NI))
    return unrows(out_e), unrows(out_h), gradient


def on_split(split):
    return jax.shard_map(
        body,
        mesh=split,
        in_specs=(P(None, XY, GZ, None),) * 4 + (P(XY, GZ, None),) * 2 + (P(),),
        out_specs=(P(None, XY, GZ, None), P(None, XY, GZ, None), P()),
        check_vma=False,
    )


def solution(mesh):
    return on_split(Mesh(mesh.devices.reshape(4, 8, 2, 2, 4), AXES))
```

```python
import functools

import jax
import jax.numpy as jnp
from jax import lax
from jax.experimental import pallas as pl
from jax.experimental.pallas import tpu as pltpu
from jax.sharding import Mesh
from jax.sharding import PartitionSpec as P

NI = 8
AXES = ("zl", "y", "c", "zh", "x")
XY = ("zl", "y", "c")
GZ = ("zh", "x")
COURANT = 0.5
ALPHA = (-COURANT, 1.0)
BETA = (1.0, -COURANT)

UP = (("ax", 10, 1, 1), ("ay", 10, 1, 2), ("px", 8, 1, 1), ("py", 8, 1, 2))
DOWN = (("sx", 11, 2, 1), ("sy", 10, 1, 1), ("qx", 9, 1, 1), ("qy", 8, 1, 1))
EARLY = 2 * 29 + 8
LATE = 2 * 10 + 1
AHEAD = 40
HALO = 13


def shift_later(u):
    lane = lax.broadcasted_iota(jnp.int32, u.shape, u.ndim - 1)
    row = lax.broadcasted_iota(jnp.int32, u.shape, u.ndim - 2)
    turned = pltpu.roll(u, 127, u.ndim - 1)
    carried = pltpu.roll(turned, 7, u.ndim - 2)
    return jnp.where(lane < 127, turned, jnp.where(row < 7, carried, 0.0))


def shift_earlier(u):
    lane = lax.broadcasted_iota(jnp.int32, u.shape, u.ndim - 1)
    row = lax.broadcasted_iota(jnp.int32, u.shape, u.ndim - 2)
    turned = pltpu.roll(u, 1, u.ndim - 1)
    carried = pltpu.roll(turned, 1, u.ndim - 2)
    return jnp.where(lane > 0, turned, jnp.where(row > 0, carried, 0.0))


def ahead_y(u):
    return shift_later(u) - u


def behind_y(u):
    return u - shift_earlier(u)


def table(material, values):
    out = jnp.zeros(material.shape, jnp.float32)
    for kind in range(4):
        out = out + jnp.where(material == kind, values[kind], 0.0)
    return out


def coefs(eps_ref):
    return [COURANT / eps_ref[kind] for kind in range(4)]


def plane(z):
    return pl.ds(z, 8, stride=2)


def keep_low(u, count, flag):
    return jnp.concatenate([u[:count] * flag, u[count:]], axis=0)


def low_flag(axes):
    first = functools.reduce(jnp.logical_and, [lax.axis_index(a) == 0 for a in axes])
    return jnp.where(first, 0.0, 1.0).astype(jnp.float32)


def pack_kernel(eps_ref, e, h, g, k, m, pair_ref, next_ref, early0, early1, eps, fields, kinds, edge, lines0, lines1, sems, outs):
    kinds_in = pltpu.make_async_copy(m, kinds, sems.at[4])
    eps_in = pltpu.make_async_copy(eps_ref, eps, sems.at[5])
    fields_in = [pltpu.make_async_copy(ref, fields.at[i], sems.at[i]) for i, ref in enumerate((e, h, g, k))]
    for copy in (kinds_in, eps_in, *fields_in):
        copy.start()
    even = lax.axis_index("c") == 0
    even_z = lax.axis_index("x") % 2 == 0
    sides = ((jnp.where(even, 6, 0), pair_ref), (jnp.where(even, 0, 6), next_ref))
    sent = []

    def send(source, target, at):
        sent.append(pltpu.make_async_copy(source, target, outs.at[at]))
        sent[-1].start()

    kinds_in.wait()
    eps_in.wait()
    values = coefs(eps)
    for side, (start, out) in enumerate(sides):
        edge[side] = table(kinds[pl.ds(start, 2)], values)
        send(edge.at[side], out.at[12], side * 5 + 4)
    for field, copy in enumerate(fields_in):
        copy.wait()
        for side, (start, out) in enumerate(sides):
            send(fields.at[field, :, pl.ds(start, 2)], out.at[3 * field : 3 * field + 3], side * 5 + field)

    coef = [table(kinds[:, plane(z), :], values) for z in range(2)]
    ups, downs = [], []
    for chain in range(2):
        alpha, beta = ALPHA[chain], BETA[chain]

        def load(field, comp, z):
            return fields[field, comp, :, plane(z), :]

        s = [[load(2 * chain, comp, z) for z in range(2)] for comp in range(3)]
        if chain == 1:
            s = [[s[comp][z] * coef[z] for z in range(2)] for comp in range(3)]
        sx, sy, sz = s
        tx, ty, tz = [], [], []
        for z in range(2):
            dz_y = sy[1] - sy[0] if z == 0 else -sy[1]
            dz_x = sx[1] - sx[0] if z == 0 else -sx[1]
            tx.append(load(2 * chain + 1, 0, z) + alpha * (ahead_y(sz[z]) - dz_y))
            ty.append(load(2 * chain + 1, 1, z)[:7] + alpha * (dz_x[:7] - (sz[z][1:] - sz[z][:7])))
            tz.append(load(2 * chain + 1, 2, z)[:7] + alpha * ((sy[z][1:] - sy[z][:7]) - ahead_y(sx[z][:7])))
        b0, b1 = beta * coef[0], beta * coef[1]
        qx = sx[0][:7] + b0[:7] * (behind_y(tz[0]) - ty[0])
        qy = sy[0][1:7] + b0[1:7] * (tx[0][1:7] - (tz[0][1:] - tz[0][:6]))
        s1x = sx[1][:7] + b1[:7] * (behind_y(tz[1]) - (ty[1] - ty[0]))
        s1y = sy[1][1:7] + b1[1:7] * ((tx[1] - tx[0])[1:7] - (tz[1][1:] - tz[1][:6]))
        s1z = sz[1][1:7] + b1[1:7] * ((ty[1][1:] - ty[1][:6]) - behind_y(tx[1][1:7]))
        px = tx[1][1:7] + alpha * (ahead_y(s1z) + s1y)
        py = ty[1][1:6] - alpha * (s1x[1:6] + (s1z[1:] - s1z[:5]))
        ups += [tx[1], ty[1], px, py, jnp.zeros((3, 8, 128), jnp.float32)]
        downs += [sx[0], sy[0], qx, qy]
        if chain == 0:
            ups.append(coef[1])
            downs.append(coef[0])
    up, down = jnp.concatenate(ups, axis=0), jnp.concatenate(downs, axis=0)
    lines1[...] = jnp.where(even_z, down, up)
    send(lines1, early1, 10)
    lines0[...] = jnp.where(even_z, up, down)[:AHEAD]
    send(lines0, early0, 11)
    for copy in sent:
        copy.wait()


def edges(planes, layout):
    picked = []
    for value, (_, count, low, high) in zip(planes, layout):
        picked += [value[:low], value[count - high :]]
    return jnp.concatenate(picked, axis=0)


def rest(planes, layout):
    inner = [value[low : count - high] for value, (_, count, low, high) in zip(planes, layout)]
    inner = jnp.concatenate(inner, axis=0)
    missing = 29 - inner.shape[0]
    if missing:
        inner = jnp.concatenate([inner, jnp.zeros((missing, 8, 128), jnp.float32)], axis=0)
    return inner[AHEAD - 37 :]


def local_kernel(eps_ref, e, h, g, kf, m, next_ref, pair_ref, late0, late1, t1s, s1s, s0s, cs):
    even_x = lax.axis_index("c") == 0
    even_z = lax.axis_index("x") % 2 == 0
    x_flag = low_flag(XY)
    values = coefs(eps_ref)

    def below(row, z):
        return jnp.where(even_x, next_ref[row // 2, row % 2, plane(z), :], pair_ref[row // 2, row % 2, plane(z), :])[None]

    def above(row, z):
        return jnp.where(even_x, pair_ref[row // 2, row % 2, plane(z), :], next_ref[row // 2, row % 2, plane(z), :])[None]

    def extended(ref, base, comp, z):
        row = base + comp * 2
        return jnp.concatenate(
            [below(row, z), below(row + 1, z), ref[comp, :, plane(z), :], above(row, z), above(row + 1, z)],
            axis=0,
        )

    coef = []
    for z in range(2):
        own = table(m[:, plane(z), :], values)
        coef.append(jnp.concatenate([below(24, z), below(25, z), own, above(24, z), above(25, z)], axis=0))
        cs[z] = coef[z][1:11]

    for chain in range(2):
        alpha, beta = ALPHA[chain], BETA[chain]
        if chain == 0:
            s = [[extended(e, 0, comp, z) for z in range(2)] for comp in range(3)]
            t = [[extended(h, 6, comp, z)[:11] for z in range(2)] for comp in range(3)]
        else:
            s = [[extended(g, 12, comp, z) * coef[z] for z in range(2)] for comp in range(3)]
            t = [[extended(kf, 18, comp, z)[:11] for z in range(2)] for comp in range(3)]
        sx, sy, sz = s
        t1 = [[None, None] for _ in range(3)]
        for z in range(2):
            dz_y = (sy[1] - sy[0])[:11] if z == 0 else -sy[1][:11]
            dz_x = (sx[1] - sx[0])[:11] if z == 0 else -sx[1][:11]
            t1[0][z] = t[0][z] + alpha * (ahead_y(sz[z][:11]) - dz_y)
            t1[1][z] = t[1][z] + alpha * (dz_x - (sz[z][1:] - sz[z][:11]))
            t1[2][z] = t[2][z] + alpha * ((sy[z][1:] - sy[z][:11]) - ahead_y(sx[z][:11]))
            for comp in range(3):
                t1[comp][z] = keep_low(t1[comp][z], 2, x_flag)
                t1s[chain, comp, z] = t1[comp][z]
        s1 = [[None, None] for _ in range(3)]
        for z in range(2):
            tx, ty, tz = t1[0][z], t1[1][z], t1[2][z]
            b = beta * coef[z][1:11]
            dz_y = ty[1:] if z == 0 else (ty - t1[1][0])[1:]
            dz_x = tx[1:] if z == 0 else (tx - t1[0][0])[1:]
            s1[0][z] = sx[z][1:11] + b * (behind_y(tz[1:]) - dz_y)
            s1[1][z] = sy[z][1:11] + b * (dz_x - (tz[1:] - tz[:10]))
            s1[2][z] = sz[z][1:11] + b * ((ty[1:] - ty[:10]) - behind_y(tx[1:]))
            for comp in range(3):
                s1s[chain, comp, z] = s1[comp][z]
        s0s[chain, 0] = sx[0][1:11]
        s0s[chain, 1] = sy[0][1:11]
        ax, ay = t1[0][1][1:], t1[1][1][1:]
        px = ax[1:9] + alpha * (ahead_y(s1[2][1][1:9]) + s1[1][1][1:9])
        py = ay[1:9] - alpha * (s1[0][1][1:9] + (s1[2][1][2:10] - s1[2][1][1:9]))
        up = (ax, ay, px, py)
        down = (sx[0][:11], sy[0][1:11], s1[0][0][:9], s1[1][0][1:9])
        late_up = edges(up, UP)
        late_down = jnp.concatenate([edges(down, DOWN), jnp.zeros((1, 8, 128), jnp.float32)], axis=0)
        late0[pl.ds(10 * chain, 10)] = jnp.where(even_z, late_up, late_down)
        late1[pl.ds(10 * chain, 10)] = jnp.where(even_z, late_down, late_up)
    late0[pl.ds(LATE, EARLY - AHEAD)] = jnp.where(even_z, rest(up, UP), rest(down, DOWN))
    late0[20] = jnp.where(even_z, coef[1][10], coef[0][1])
    late1[20] = jnp.where(even_z, coef[0][1], coef[1][10])


def take_kernel(*refs):
    del refs


def final_kernel(eps_ref, e, g, m, owner, early1, early0, late1, late0, t1s, s1s, s0s, cs, adj_e, adj_h, sums, new_e, new_h, outs):
    even_z = lax.axis_index("x") % 2 == 0
    x_flag, z_flag = low_flag(XY), low_flag(GZ)
    values = coefs(eps_ref)
    inverse = [2.0 * eps_ref[kind] for kind in range(4)]

    def early_even(start, count):
        ahead = max(0, min(count, AHEAD - start))
        parts = [early0[pl.ds(start, ahead)]] if ahead else []
        if ahead < count:
            parts.append(late0[pl.ds(LATE + start + ahead - AHEAD, count - ahead)])
        return jnp.concatenate(parts, axis=0)

    def early_up(start, count):
        return jnp.where(even_z, early_even(start, count), early1[pl.ds(start, count)])

    def early_low(start, count):
        return jnp.where(even_z, early1[pl.ds(start, count)], early_even(start, count))

    def late_up(start, count):
        return jnp.where(even_z, late0[pl.ds(start, count)], late1[pl.ds(start, count)])

    def late_low(start, count):
        return jnp.where(even_z, late1[pl.ds(start, count)], late0[pl.ds(start, count)])

    def joined(early_lines, late_lines, layout, chain, at):
        first, edge = 37 * chain, 10 * chain
        for _, count, low, high in layout[:at]:
            first, edge = first + count - low - high, edge + low + high
        _, count, low, high = layout[at]
        middle = early_lines(first, count - low - high)
        return jnp.concatenate([late_lines(edge, low), middle, late_lines(edge + low, high)], axis=0)

    c_up = jnp.concatenate([late_up(20, 1), early_up(29, 8)], axis=0)
    c_low = jnp.concatenate([early_low(29, 8), late_low(20, 1)], axis=0)
    own = slice(1, 9)
    kept = [None, None]
    writes = [pltpu.make_async_copy(new_e, adj_e, outs.at[0]), pltpu.make_async_copy(new_h, adj_h, outs.at[1])]
    for chain in (1, 0):
        alpha, beta = ALPHA[chain], BETA[chain]
        sx2, sy2, qx, qy = (joined(early_up, late_up, DOWN, chain, at) for at in range(4))
        ax, ay, px, py = (joined(early_low, late_low, UP, chain, at) for at in range(4))
        sx0, sy0 = s0s[chain, 0], s0s[chain, 1]
        tx = [t1s[chain, 0, 0][1:], t1s[chain, 0, 1][1:] - alpha * sy2]
        ty = [t1s[chain, 1, 0][1:], t1s[chain, 1, 1][1:] + alpha * sx2[1:]]
        tz = [t1s[chain, 2, 0][1:], t1s[chain, 2, 1][1:]]
        tx_low = (ax - alpha * sy0) * z_flag
        ty_low = (ay + alpha * sx0) * z_flag
        b0, b1 = beta * cs[0], beta * cs[1]
        div2 = (sx2[1:] - sx2[:10]) + behind_y(sy2)
        sx = [s1s[chain, 0, 0] + b0 * ty_low, s1s[chain, 0, 1] - alpha * b1 * sx2[1:]]
        sy = [s1s[chain, 1, 0] - b0 * tx_low, s1s[chain, 1, 1] - alpha * b1 * sy2]
        sz = [s1s[chain, 2, 0], s1s[chain, 2, 1] + alpha * b1 * div2]
        b_up, b_low = beta * c_up, beta * c_low
        sx.append(qx + b_up * ty[1][:9])
        sy_top = qy - b_up[1:] * tx[1][own]
        t2x, t2y, t2z = [], [], []
        for z in range(2):
            dz_y = (sy[1] - sy[0])[own] if z == 0 else sy_top - sy[1][own]
            dz_x = sx[z + 1][:9] - sx[z][:9]
            t2x.append(tx[z][own] + alpha * (ahead_y(sz[z][own]) - dz_y))
            y_new = ty[z][:9] + alpha * (dz_x - (sz[z][1:] - sz[z][:9]))
            z_new = tz[z][:9] + alpha * ((sy[z][1:] - sy[z][:9]) - ahead_y(sx[z][:9]))
            t2y.append(keep_low(y_new, 1, x_flag))
            t2z.append(keep_low(z_new, 1, x_flag))
        div0 = b_low * ((sx0[1:] - sx0[:9]) + behind_y(sy0[1:]))
        x_low = px - alpha * (sy0[own] + sy[0][own]) + alpha * alpha * (ahead_y(div0[:8]) - b_low[:8] * sy0[own])
        y_low = py + alpha * (sx0[own] + sx[0][own]) + alpha * alpha * (b_low[:8] * sx0[own] - (div0[1:] - div0[:8]))
        x_low, y_low = x_low * z_flag, y_low * z_flag
        curl = []
        for z in range(2):
            dz_y = t2y[z][1:] - (y_low if z == 0 else t2y[0][1:])
            dz_x = t2x[z] - (x_low if z == 0 else t2x[0])
            curl.append((
                behind_y(t2z[z][1:]) - dz_y,
                dz_x - (t2z[z][1:] - t2z[z][:8]),
                (t2y[z][1:] - t2y[z][:8]) - behind_y(t2x[z]),
            ))
        kept[chain] = ([[s[z][own] for s in (sx, sy, sz)] for z in range(2)], curl)
        if chain == 1:
            for z in range(2):
                scale = table(m[:, plane(z), :], inverse)
                for comp, t2 in enumerate((t2x[z], t2y[z][1:], t2z[z][1:])):
                    new_e[comp, :, plane(z), :] = kept[1][0][z][comp] * scale - COURANT * curl[z][comp]
                    new_h[comp, :, plane(z), :] = t2
            for copy in writes:
                copy.start()

    totals = [jnp.zeros((8, 128), jnp.float32) for _ in range(NI)]
    for z in range(2):
        coef = table(m[:, plane(z), :], values)
        weight = jnp.zeros((8, 8, 128), jnp.float32)
        for comp in range(3):
            step = kept[0][0][z][comp] - e[comp, :, plane(z), :]
            weight = weight + kept[1][0][z][comp] * step
            weight = weight + coef * g[comp, :, plane(z), :] * (coef * kept[0][1][z][comp])
        who = owner[:, plane(z), :]
        for j in range(NI):
            totals[j] = totals[j] + jnp.sum(jnp.where(who == j, weight, 0.0), axis=0)
    lane = lax.broadcasted_iota(jnp.int32, (1, 128), 1)
    row = jnp.zeros((1, 128), jnp.float32)
    for j in range(NI):
        row = row + jnp.where(lane == j, jnp.sum(totals[j]), 0.0)
    sums[...] = jnp.broadcast_to(row, sums.shape)
    for copy in writes:
        copy.wait()


VMEM = pl.BlockSpec(memory_space=pltpu.VMEM)
SMEM = pl.BlockSpec(memory_space=pltpu.SMEM)
ANY = pl.BlockSpec(memory_space=pl.ANY)
HBM = pl.BlockSpec(memory_space=pltpu.HBM)
TAKE = 2 * 10**10
LARGE = 62 * 1024 * 1024
PARAMS = pltpu.CompilerParams(vmem_limit_bytes=48 * 1024 * 1024)


def f32(*shape):
    return jax.ShapeDtypeStruct(shape, jnp.float32)


def rows(u):
    lead = u.shape[:-2]
    n = len(lead)
    return u.reshape(*lead, 2, 8, 128).transpose(*range(n), n + 1, n, n + 2).reshape(*lead, 16, 128)


def unrows(u):
    lead = u.shape[:-2]
    n = len(lead)
    return u.reshape(*lead, 8, 2, 128).transpose(*range(n), n + 1, n, n + 2).reshape(*lead, 2, 1024)


def swap_pairs(value, axes, odd):
    size = lax.axis_size(axes)
    pairs = []
    for low in range(odd, size - 1, 2):
        pairs += [(low, low + 1), (low + 1, low)]
    return lax.ppermute(value, axes, pairs)


def spread_sum(value, axes):
    size = lax.axis_size(axes)
    sent = jnp.broadcast_to(value[None], (size, value.shape[0]))
    return jnp.sum(lax.all_to_all(sent, axes, 0, 0), axis=0)


def body(e_check, h_check, adj_e, adj_h, material, owner, permittivity):
    e, h, g, k, m, own = (rows(u) for u in (e_check, h_check, adj_e, adj_h, material, owner))
    pair, following, early0, early1 = pl.pallas_call(
        pack_kernel,
        out_shape=(f32(HALO, 2, 16, 128), f32(HALO, 2, 16, 128), f32(AHEAD, 8, 128), f32(EARLY, 8, 128)),
        in_specs=[HBM] * 6,
        out_specs=[HBM] * 4,
        scratch_shapes=[
            pltpu.SMEM((4,), jnp.float32),
            pltpu.VMEM((4, 3, 8, 16, 128), jnp.float32),
            pltpu.VMEM((8, 16, 128), jnp.int32),
            pltpu.VMEM((2, 2, 16, 128), jnp.float32),
            pltpu.VMEM((AHEAD, 8, 128), jnp.float32),
            pltpu.VMEM((EARLY, 8, 128), jnp.float32),
            pltpu.SemaphoreType.DMA((6,)),
            pltpu.SemaphoreType.DMA((12,)),
        ],
        compiler_params=pltpu.CompilerParams(vmem_limit_bytes=LARGE),
        name="pack",
    )(permittivity, e, h, g, k, m)
    early1 = swap_pairs(early1, GZ, 1)
    early0 = swap_pairs(early0, "x", 0)
    pair = swap_pairs(pair, "c", 0)
    following = swap_pairs(following, XY, 1)
    late0, late1, t1s, s1s, s0s, cs = pl.pallas_call(
        local_kernel,
        out_shape=(
            f32(LATE + EARLY - AHEAD, 8, 128),
            f32(LATE, 8, 128),
            f32(2, 3, 2, 11, 8, 128),
            f32(2, 3, 2, 10, 8, 128),
            f32(2, 2, 10, 8, 128),
            f32(2, 10, 8, 128),
        ),
        in_specs=[SMEM] + [VMEM] * 7,
        out_specs=[VMEM] * 6,
        compiler_params=PARAMS,
        cost_estimate=pl.CostEstimate(flops=1, bytes_accessed=1, transcendentals=0),
        name="local_step",
    )(permittivity, e, h, g, k, m, following, pair)
    late0 = swap_pairs(late0, "x", 0)
    late1 = swap_pairs(late1, GZ, 1)
    early1, early0 = pl.pallas_call(
        take_kernel,
        out_shape=(f32(EARLY, 8, 128), f32(AHEAD, 8, 128)),
        in_specs=[ANY] * 2,
        out_specs=[ANY] * 2,
        input_output_aliases={0: 0, 1: 1},
        compiler_params=PARAMS,
        cost_estimate=pl.CostEstimate(flops=TAKE, bytes_accessed=10**9, transcendentals=0),
        name="take_early",
    )(early1, early0)
    out_e, out_h, sums = pl.pallas_call(
        final_kernel,
        out_shape=(f32(3, 8, 16, 128), f32(3, 8, 16, 128), f32(lax.axis_size(("zl", "zh", "c")), 128)),
        in_specs=[SMEM] + [VMEM] * 12,
        out_specs=[HBM, HBM, VMEM],
        scratch_shapes=[
            pltpu.VMEM((3, 8, 16, 128), jnp.float32),
            pltpu.VMEM((3, 8, 16, 128), jnp.float32),
            pltpu.SemaphoreType.DMA((2,)),
        ],
        compiler_params=PARAMS,
        name="final_step",
    )(permittivity, e, g, m, own, early1, early0, late1, late0, t1s, s1s, s0s, cs)
    total = jnp.sum(lax.all_to_all(sums, ("zl", "zh", "c"), 0, 0, tiled=True), axis=0)
    total = spread_sum(total, ("y", "x"))
    cells = 8 * lax.axis_size(XY) * 2 * lax.axis_size(GZ) * 1024
    gradient = total[:NI] / jnp.sqrt(jnp.float32(cells / NI))
    return unrows(out_e), unrows(out_h), gradient


def on_split(split):
    return jax.shard_map(
        body,
        mesh=split,
        in_specs=(P(None, XY, GZ, None),) * 4 + (P(XY, GZ, None),) * 2 + (P(),),
        out_specs=(P(None, XY, GZ, None), P(None, XY, GZ, None), P()),
        check_vma=False,
    )


def solution(mesh):
    return on_split(Mesh(mesh.devices.reshape(4, 8, 2, 2, 4), AXES))
```
